128 devices in a mesh: lon: 16 (over z, y_lo, core), lat: 8 (over x, y_hi).
Axes of the slice: x: 4, y: 4 (y_hi: 2, y_lo: 2; y = y_hi * 2 + y_lo), z: 4, core: 2. Of those that a mesh axis runs over, the one named last changes fastest.
Arguments:
- frames: bfloat16 [1, 1, 16, 2048, 1024], P(None, None, None, 'lon', 'lat'), may hold values from -6 to 6
- hidden_low: bfloat16 [1, 64, 2048, 1024], P(None, None, 'lon', 'lat'), may hold values from -0.8984375 to 0.8984375
- cell_low: float32 [1, 64, 2048, 1024], P(None, None, 'lon', 'lat'), may hold values from -4 to 4
- hidden_top: bfloat16 [1, 64, 2048, 1024], P(None, None, 'lon', 'lat'), may hold values from -0.8984375 to 0.8984375
- cell_top: float32 [1, 64, 2048, 1024], P(None, None, 'lon', 'lat'), may hold values from -4 to 4
- weight_low: bfloat16 [256, 720], replicated, may hold values from -0.21875 to 0.21875
- bias_low: float32 [256], replicated, may hold values from -3 to 3
- weight_top: bfloat16 [256, 1152], replicated, may hold values from -0.1875 to 0.1875
- bias_top: float32 [256], replicated, may hold values from -3 to 3
Outputs:
- top_states: bfloat16 [1, 1, 64, 2048, 1024], P(None, None, None, 'lon', 'lat')
- hidden_low_out: bfloat16 [1, 64, 2048, 1024], P(None, None, 'lon', 'lat')
- cell_low_out: float32 [1, 64, 2048, 1024], P(None, None, 'lon', 'lat')
- cell_top_out: float32 [1, 64, 2048, 1024], P(None, None, 'lon', 'lat')
The draws below stay inside these ranges and needn't reach their ends.
All inputs are finite; a program needn't handle non-finite values.
Results may differ from the reference program's by a relative error of at most 0.0017.
Values may be sent and summed in bfloat16 or wider, within the bound.
A program may use at most 384 MiB of HBM per device.

```python
import jax
import jax.numpy as jnp
from jax import lax

CIN = 16
HID = 64
FRAMES = 1
BATCH = 1
NLON = 2048
NLAT = 1024


def level_of(own_key, shape, cuts, low, largest):
    factor_of = 1.0
    for axis_at, blocks in cuts:
        heights = jax.random.uniform(jax.random.fold_in(jax.random.fold_in(own_key, 6), axis_at), (blocks,), jnp.float32, low / len(cuts), largest / len(cuts))
        factor_of = factor_of * jnp.repeat(jnp.exp(heights), shape[axis_at] // blocks).reshape((-1,) + (1,) * (len(shape) - 1 - axis_at))
    return factor_of


def gaussian(stream_key, dims, scale, most, cuts=(), kind=jnp.bfloat16):
    entries = jax.random.normal(stream_key, dims, jnp.float32) * scale
    if len(cuts) > 0:
        entries = level_of(stream_key, dims, cuts, -0.22, 0.18) * entries
    return jnp.clip(entries, min=-most, max=most).astype(kind)


def setup_inputs(seed: int = 0) -> dict:
    keys = jax.random.split(jax.random.key(seed), 10)
    return {
        "frames": gaussian(keys[0], (FRAMES, BATCH, CIN, NLON, NLAT), 1.0, 6.0, ((3, 16), (4, 8))),
        "hidden_low": jnp.clip(jax.random.uniform(keys[1], (BATCH, HID, NLON, NLAT), jnp.float32, -0.8984375, 0.8984375) * level_of(keys[1], (BATCH, HID, NLON, NLAT), ((2, 16), (3, 8)), -0.4, 0.0), -0.8984375, 0.8984375).astype(jnp.bfloat16),
        "cell_low": gaussian(keys[2], (BATCH, HID, NLON, NLAT), 1.0, 4.0, ((2, 16), (3, 8)), jnp.float32),
        "hidden_top": jnp.clip(jax.random.uniform(keys[3], (BATCH, HID, NLON, NLAT), jnp.float32, -0.8984375, 0.8984375) * level_of(keys[3], (BATCH, HID, NLON, NLAT), ((2, 16), (3, 8)), -0.4, 0.0), -0.8984375, 0.8984375).astype(jnp.bfloat16),
        "cell_top": gaussian(keys[4], (BATCH, HID, NLON, NLAT), 1.0, 4.0, ((2, 16), (3, 8)), jnp.float32),
        "weight_low": gaussian(keys[5], (4 * HID, 9 * (CIN + HID)), (9 * (CIN + HID)) ** -0.5, 0.21875),
        "bias_low": gaussian(keys[6], (4 * HID,), 1.0, 3.0, (), jnp.float32),
        "weight_top": gaussian(keys[7], (4 * HID, 9 * 2 * HID), (9 * 2 * HID) ** -0.5, 0.1875),
        "bias_top": gaussian(keys[8], (4 * HID,), 1.0, 3.0, (), jnp.float32),
    }


def pad_field(field):
    lon_total = field.shape[2]
    rolled = jnp.roll(field, lon_total // 2, axis=2)
    lat_padded = jnp.concatenate([rolled[..., :1], field, rolled[..., -1:]], axis=3)
    return jnp.concatenate([lat_padded[:, :, -1:], lat_padded, lat_padded[:, :, :1]], axis=2)


def columns(padded, lon_total, lat_total):
    pieces = []
    for lon_off in range(3):
        for lat_off in range(3):
            pieces.append(padded[:, :, lon_off:lon_off + lon_total, lat_off:lat_off + lat_total])
    return jnp.concatenate(pieces, axis=1)


def gate_update(cols, weight, bias, cell_prev):
    gates = jnp.einsum("ok,bkxy->boxy", weight.astype(jnp.float32), cols.astype(jnp.float32))
    gates = gates + bias[None, :, None, None]
    in_gate, forget_gate, candidate, out_gate = jnp.split(gates, 4, axis=1)
    cell_new = jax.nn.sigmoid(forget_gate) * cell_prev + jax.nn.sigmoid(in_gate) * jnp.tanh(candidate)
    hidden_new = (jax.nn.sigmoid(out_gate) * jnp.tanh(cell_new)).astype(jnp.bfloat16)
    return hidden_new, cell_new


def reference(frames, hidden_low, cell_low, hidden_top, cell_top, weight_low, bias_low, weight_top, bias_top):
    lon_total = frames.shape[3]
    lat_total = frames.shape[4]

    def advance(state_carry, frame):
        low_h, low_c, top_h, top_c = state_carry
        input_low = jnp.concatenate([frame, low_h], axis=1)
        low_h, low_c = gate_update(columns(pad_field(input_low), lon_total, lat_total), weight_low, bias_low, low_c)
        input_top = jnp.concatenate([low_h, top_h], axis=1)
        top_h, top_c = gate_update(columns(pad_field(input_top), lon_total, lat_total), weight_top, bias_top, top_c)
        return (low_h, low_c, top_h, top_c), top_h

    final_state, top_states = lax.scan(advance, (hidden_low, cell_low, hidden_top, cell_top), frames)
    return (top_states, final_state[0], final_state[1], final_state[3])
```

```python
import functools

import jax
import jax.numpy as jnp
from jax import lax
from jax.experimental import pallas as pl
from jax.experimental.pallas import tpu as pltpu
from jax.sharding import PartitionSpec as P

CIN, HID, TILE, BX = 16, 64, 128, 16
CL = CIN + HID
CT = 2 * HID
NB = TILE // BX
PK = 2 * CL + HID
F32, BF16 = jnp.float32, jnp.bfloat16
MESH = pl.DeviceIdType.MESH


def rot(block, shift):
    return pltpu.roll(block, shift % block.shape[1] if isinstance(shift, int) else shift, 1)


def lanes(shape):
    return lax.broadcasted_iota(jnp.int32, shape, 1)


def exchange_kernel(
    fr, hl, ht, cl,
    latb, latf, lonb, lonf, own,
    frv, hlv, htv, clv, tmp, sb, sf, lb, lf,
    in_sem, send_lat, recv_lat, send_lon, recv_lon,
):
    nlon, nlat = lax.axis_size("lon"), lax.axis_size("lat")
    lon, lat = lax.axis_index("lon"), lax.axis_index("lat")
    loads = [
        pltpu.make_async_copy(src, dst, in_sem.at[k])
        for k, (src, dst) in enumerate(((fr, frv), (hl, hlv), (ht, htv), (cl, clv)))
    ]
    for load in loads:
        load.start()

    sides = []
    for side in range(2):
        polar = lat == (0 if side == 0 else nlat - 1)
        to_lat = jnp.where(polar, lat, lat + (-1 if side == 0 else 1))
        shift = jnp.where(polar, nlon // 2, 0)
        slot = jnp.where(polar, side, 1 - side)
        sides.append((to_lat, shift, slot))
    lat_targets = [
        [(lax.rem(lon + shift + step + nlon, nlon), to_lat) for step in (-1, 0, 1)]
        for to_lat, shift, _ in sides
    ]
    lon_targets = [(lax.rem(lon + step + nlon, nlon), lat) for step in (-1, 1)]

    barrier = pltpu.get_barrier_semaphore()
    for target in lat_targets[0] + lat_targets[1] + lon_targets:
        pl.semaphore_signal(barrier, inc=1, device_id=target, device_id_type=MESH)

    row = lax.broadcasted_iota(jnp.int32, (16, TILE), 0)
    col = lax.broadcasted_iota(jnp.int32, (16, TILE), 1)
    wanted = jnp.where(row == 1, 1, jnp.where(row == 2, TILE - 1, jnp.where(row == 3, TILE - 2, 0)))
    pick = jnp.where((col == wanted) & (row < 4), 1.0, 0.0).astype(BF16)
    dims = (((1,), (1,)), ((), ()))

    def columns(field, base, count):
        def step(k, carry):
            at = pl.multiple_of(k * 8, 8)
            found = lax.dot_general(
                pick, field[pl.ds(at, 8)].reshape(8 * TILE, TILE), dims, preferred_element_type=F32
            )
            for j in range(8):
                tmp[pl.ds(pl.multiple_of((base + at + j) * 8, 8), 8), :] = found[0:8, j * TILE:(j + 1) * TILE]
            return carry
        lax.fori_loop(0, count // 8, step, 0)

    def rows(field, count, base, whole):
        for side in range(2):
            start = 0 if side == 0 else TILE - BX
            tmp[0:count * BX, :] = field[:, start:start + BX, :].astype(F32).reshape(count * BX, TILE)
            near, far = (0, 1) if side == 0 else (BX - 1, BX - 2)
            if whole:
                lb[side, base:base + count] = tmp[pl.ds(near, count, stride=BX), :].astype(BF16)
                lb[side, CL + base:CL + base + count] = tmp[pl.ds(far, count, stride=BX), :].astype(BF16)
            else:
                lb[side, 2 * CL:2 * CL + count] = tmp[pl.ds(near, count, stride=BX), :].astype(BF16)

    loads[0].wait()
    rows(frv, CIN, 0, True)
    loads[1].wait()
    rows(hlv, HID, CIN, True)
    columns(frv, 0, CIN)
    columns(hlv, CIN, HID)
    for side in range(2):
        near = tmp[pl.ds(2 * side, CL, stride=8), :].astype(BF16)
        sb[side, 0:CL] = near
        own[side] = near
        sb[side, CL:2 * CL] = tmp[pl.ds(2 * side + 1, CL, stride=8), :].astype(BF16)
    loads[2].wait()
    rows(htv, HID, 0, False)
    columns(htv, 0, HID)
    for side in range(2):
        sb[side, 2 * CL:PK] = tmp[pl.ds(2 * side, HID, stride=8), :].astype(BF16)

    pl.semaphore_wait(barrier, 8)

    copies = []

    def send(kind, lat_src, lat_dst, lon_src, lon_dst):
        for side in range(2):
            for pos in range(3):
                slot = sides[side][2]
                copies.append(pltpu.make_async_remote_copy(
                    src_ref=lat_src.at[side], dst_ref=lat_dst.at[slot, 2 - pos],
                    send_sem=send_lat.at[kind, side, pos], recv_sem=recv_lat.at[kind, slot, 2 - pos],
                    device_id=lat_targets[side][pos], device_id_type=MESH))
                copies[-1].start()
            copies.append(pltpu.make_async_remote_copy(
                src_ref=lon_src.at[side], dst_ref=lon_dst.at[1 - side],
                send_sem=send_lon.at[kind, side], recv_sem=recv_lon.at[kind, 1 - side],
                device_id=lon_targets[side], device_id_type=MESH))
            copies[-1].start()

    send(0, sb, latb, lb, lonb)

    loads[3].wait()

    def cell_columns(k, carry):
        at = pl.multiple_of(k * 8, 8)
        block = clv[pl.ds(at, 8)].reshape(8 * TILE, TILE)
        high = block.astype(BF16)
        rest = block - high.astype(F32)
        mid = rest.astype(BF16)
        low = (rest - mid.astype(F32)).astype(BF16)
        found = lax.dot_general(pick, high, dims, preferred_element_type=F32)
        found += lax.dot_general(pick, mid, dims, preferred_element_type=F32)
        found += lax.dot_general(pick, low, dims, preferred_element_type=F32)
        for j in range(8):
            tmp[pl.ds(pl.multiple_of((at + j) * 8, 8), 8), :] = found[0:8, j * TILE:(j + 1) * TILE]
        return carry

    lax.fori_loop(0, HID // 8, cell_columns, 0)
    for side in range(2):
        sf[side] = tmp[pl.ds(2 * side, HID, stride=8), :]
    for side in range(2):
        start, near = (0, 0) if side == 0 else (TILE - 8, 7)
        tmp[0:HID * 8, :] = clv[:, start:start + 8, :].reshape(HID * 8, TILE)
        lf[side] = tmp[pl.ds(near, HID, stride=8), :]
    send(1, sf, latf, lf, lonf)

    for kind, lat_dst, lon_dst, lat_src, lon_src in ((0, latb, lonb, sb, lb), (1, latf, lonf, sf, lf)):
        for slot in range(2):
            for pos in range(3):
                pltpu.make_async_remote_copy(
                    src_ref=lat_src.at[0], dst_ref=lat_dst.at[slot, pos],
                    send_sem=send_lat.at[kind, slot, pos], recv_sem=recv_lat.at[kind, slot, pos],
                    device_id=lat_targets[0][0], device_id_type=MESH).wait_recv()
            pltpu.make_async_remote_copy(
                src_ref=lon_src.at[0], dst_ref=lon_dst.at[slot],
                send_sem=send_lon.at[kind, slot], recv_sem=recv_lon.at[kind, slot],
                device_id=lon_targets[0], device_id_type=MESH).wait_recv()
    for copy in copies:
        copy.wait_send()


def exchange(fr, hl, ht, cl):
    whole = pl.BlockSpec(memory_space=pltpu.VMEM)
    return pl.pallas_call(
        exchange_kernel,
        out_shape=(
            jax.ShapeDtypeStruct((2, 3, PK, TILE), BF16),
            jax.ShapeDtypeStruct((2, 3, HID, TILE), F32),
            jax.ShapeDtypeStruct((2, PK, TILE), BF16),
            jax.ShapeDtypeStruct((2, HID, TILE), F32),
            jax.ShapeDtypeStruct((2, CL, TILE), BF16),
        ),
        in_specs=[pl.BlockSpec(memory_space=pl.ANY)] * 4,
        out_specs=(whole,) * 5,
        scratch_shapes=[
            pltpu.VMEM((CIN, TILE, TILE), BF16),
            pltpu.VMEM((HID, TILE, TILE), BF16),
            pltpu.VMEM((HID, TILE, TILE), BF16),
            pltpu.VMEM((HID, TILE, TILE), F32),
            pltpu.VMEM((HID * BX, TILE), F32),
            pltpu.VMEM((2, PK, TILE), BF16),
            pltpu.VMEM((2, HID, TILE), F32),
            pltpu.VMEM((2, PK, TILE), BF16),
            pltpu.VMEM((2, HID, TILE), F32),
            pltpu.SemaphoreType.DMA((4,)),
            pltpu.SemaphoreType.DMA((2, 2, 3)),
            pltpu.SemaphoreType.DMA((2, 2, 3)),
            pltpu.SemaphoreType.DMA((2, 2)),
            pltpu.SemaphoreType.DMA((2, 2)),
        ],
        compiler_params=pltpu.CompilerParams(
            collective_id=0, has_side_effects=True, vmem_limit_bytes=32 * 1024 * 1024
        ),
        name="halo_exchange",
    )(fr, hl, ht, cl)


def update(gates, cell):
    take = jnp.tanh(gates[0:HID])
    keep = jnp.tanh(gates[HID:2 * HID])
    cand = jnp.tanh(gates[2 * HID:3 * HID])
    show = jnp.tanh(gates[3 * HID:4 * HID])
    cell = 0.5 * ((keep + 1.0) * cell + (take + 1.0) * cand)
    return 0.5 * (show + 1.0) * jnp.tanh(cell), cell


def extended_weights(out, weight, bias, width):
    gate = lax.broadcasted_iota(jnp.int32, (4 * HID, 1), 0)
    half = jnp.where((gate >= 2 * HID) & (gate < 3 * HID), 1.0, 0.5)
    out[:, 0:width] = (weight * half).astype(BF16)
    spread = jnp.transpose(jnp.broadcast_to(bias, (TILE, 4 * HID))) * half
    high = spread.astype(BF16).astype(F32)
    mid = (spread - high).astype(BF16).astype(F32)
    low = spread - high - mid
    lane = lanes((4 * HID, TILE))
    tail = jnp.where(lane == 0, high, jnp.where(lane == 1, mid, jnp.where(lane == 2, low, 0.0)))
    out[:, width:width + 16] = tail[:, 0:16].astype(BF16)


def layers_kernel(
    fr, hl, cl, ht, ct, wl, bl, wt, bt, latb, latf, lonb, lonf, own,
    th, ho, co, cto,
    frv, hlv, htv, clv, ctv, s_low, s_top, strip, hs, g_low, g_top, wle, wte, tmp,
    sem_in, sem_out,
):
    nlat = lax.axis_size("lat")
    lat = lax.axis_index("lat")

    def piece(hbm, b):
        return hbm.at[:, pl.ds(pl.multiple_of(b * BX, BX), BX), :]

    ins = ((fr, frv), (hl, hlv), (ht, htv), (cl, clv), (ct, ctv))

    def load(k, b):
        return pltpu.make_async_copy(piece(ins[k][0], b), ins[k][1].at[b], sem_in.at[k, b])

    outs = ((ho, hlv), (th, htv), (co, clv), (cto, ctv))

    def save(k, b):
        return pltpu.make_async_copy(outs[k][1].at[b], piece(outs[k][0], b), sem_out.at[k, b])

    for k in range(5):
        for b in range(NB):
            load(k, b).start()

    extended_weights(wle, jnp.transpose(wl[...].astype(F32)), bl[...], 9 * CL)
    extended_weights(wte, wt[...].astype(F32), bt[...], 9 * CT)
    ones = jnp.ones((16, 2 * TILE), BF16)

    def place(dest, at, base, width, stride, value, lane_lo, lane_hi):
        lane = lanes(value.shape)
        down = jnp.where(lane == 0, lane_lo, rot(value, 1))
        up = jnp.where(lane == TILE - 1, lane_hi, rot(value, TILE - 1))
        dest[at, base:base + width] = down.astype(BF16)
        dest[at, stride + base:stride + base + width] = value.astype(BF16)
        dest[at, 2 * stride + base:2 * stride + base + width] = up.astype(BF16)

    def interleave(dest, low, high, base, width):
        lane = lanes(low.shape)
        even = lax.rem(lane, 2) == 0
        high = rot(high, TILE - 1)
        dest[0, base:base + width] = jnp.where(even, low, high)
        dest[1, base:base + width] = jnp.where(even, high, low)

    for at, side, far in ((1, 0, 0), (0, 0, 1), (130, 1, 0), (131, 1, 1)):
        value = lonb[side, far * CL:far * CL + CL].astype(F32)
        src = (TILE - 1 - far) if side == 0 else far
        lo = rot(latb[0, 2 * side, 0:CL].astype(F32), TILE - src)
        hi = rot(latb[1, 2 * side, 0:CL].astype(F32), 2 * TILE - 1 - src)
        place(s_low, at, 0, CL, CL, value, lo, hi)
    for at, side in ((0, 0), (129, 1)):
        value = lonb[side, 2 * CL:PK].astype(F32)
        src = TILE - 1 if side == 0 else 0
        lo = rot(latb[0, 2 * side, 2 * CL:PK].astype(F32), TILE - src)
        hi = rot(latb[1, 2 * side, 2 * CL:PK].astype(F32), 2 * TILE - 1 - src)
        place(s_top, at, HID, HID, CT, value, lo, hi)
    interleave(g_low, latb[0, 1, 0:CL].astype(F32), latb[1, 1, 0:CL].astype(F32), 0, CL)
    interleave(g_top, latb[0, 1, 2 * CL:PK].astype(F32), latb[1, 1, 2 * CL:PK].astype(F32), HID, HID)

    def relayout(b, carry):
        for k in range(3):
            load(k, b).wait()
        tmp[0:CIN * BX, :] = frv[b].astype(F32).reshape(CIN * BX, TILE)
        tmp[CIN * BX:CL * BX, :] = hlv[b].astype(F32).reshape(HID * BX, TILE)
        tmp[CL * BX:(CL + HID) * BX, :] = htv[b].astype(F32).reshape(HID * BX, TILE)
        for i in range(BX):
            x = b * BX + i
            back = lax.rem(TILE - x, TILE)
            value = tmp[pl.ds(i, CL, stride=BX), :]
            halo = rot(g_low[i % 2], back)
            place(s_low, x + 2, 0, CL, CL, value, halo, halo)
            value = tmp[pl.ds(CL * BX + i, HID, stride=BX), :]
            halo = rot(g_top[i % 2, HID:CT], back)
            place(s_top, x + 1, HID, HID, CT, value, halo, halo)
        return carry

    lax.fori_loop(0, NB, relayout, 0)

    for side in range(2):
        near = jnp.concatenate([latb[side, k, 0:CL].astype(F32) for k in range(3)], axis=1)
        far = jnp.concatenate([latb[side, k, CL:2 * CL].astype(F32) for k in range(3)], axis=1)
        edge = 0 if side == 0 else TILE - 1
        lane = lanes((CL, TILE))
        parts = [lonb[0, 0:CL], lonb[0, CL:2 * CL], lonb[1, 0:CL], lonb[1, CL:2 * CL]]
        parts = [part.astype(F32) for part in parts]
        west = jnp.where(lane == TILE - 1, rot(parts[0], TILE - 1 - edge), rot(parts[1], 2 * TILE - 2 - edge))
        east = jnp.where(lane == 0, rot(parts[2], TILE - edge), rot(parts[3], TILE + 1 - edge))
        mine = jnp.concatenate([west, own[side].astype(F32), east], axis=1)
        polar = lat == (0 if side == 0 else nlat - 1)
        outer = jnp.where(polar, mine, far)
        inner = jnp.where(polar, far, mine)
        order = (outer, near, inner) if side == 0 else (inner, near, outer)
        for e in range(3):
            for a in range(3):
                at = (3 * a + e) * CL
                strip[at:at + CL, :] = rot(order[e], 1 - a).astype(BF16)
        gates = jnp.dot(
            wle[:, 0:9 * CL + 16],
            jnp.concatenate([strip[...], jnp.ones((16, 3 * TILE), BF16)], axis=0),
            preferred_element_type=F32,
        )
        cell = jnp.concatenate([latf[side, k] for k in range(3)], axis=1)
        hs[side], _ = update(gates, cell)
    interleave(g_top, hs[0, :, TILE:2 * TILE], hs[1, :, TILE:2 * TILE], 0, HID)

    def windows(source, first, second, width, weights):
        pair = jnp.concatenate(
            [source[pl.ds(first, 3)].reshape(width, TILE), source[pl.ds(second, 3)].reshape(width, TILE)], axis=1
        )
        return jnp.dot(
            weights[:, 0:width + 16], jnp.concatenate([pair, ones], axis=0), preferred_element_type=F32
        )

    hidden, _ = update(
        windows(s_low, 0, 129, 9 * CL, wle), jnp.concatenate([lonf[0], lonf[1]], axis=1)
    )
    for side, at in ((0, 0), (1, 129)):
        src = TILE - 1 if side == 0 else 0
        lo = rot(hs[0, :, 2 * side * TILE:(2 * side + 1) * TILE], TILE - src)
        hi = rot(hs[1, :, 2 * side * TILE:(2 * side + 1) * TILE], 2 * TILE - 1 - src)
        place(s_top, at, 0, HID, CT, hidden[:, side * TILE:(side + 1) * TILE], lo, hi)

    def low_block(b, carry):
        load(3, b).wait()
        cells = clv.at[b].reshape(HID * BX, TILE)
        for i in range(0, BX, 2):
            x = b * BX + i
            cell = jnp.concatenate([cells[pl.ds(i + j, HID, stride=BX), :] for j in range(2)], axis=1)
            hidden, cell = update(windows(s_low, x + 1, x + 2, 9 * CL, wle), cell)
            for j in range(2):
                part = slice(j * TILE, (j + 1) * TILE)
                cells[pl.ds(i + j, HID, stride=BX), :] = cell[:, part]
                tmp[pl.ds(i + j, HID, stride=BX), :] = hidden[:, part]
                halo = rot(g_top[j, 0:HID], lax.rem(TILE - x - j, TILE))
                place(s_top, x + j + 1, 0, HID, CT, hidden[:, part], halo, halo)
        hlv[b] = tmp[0:HID * BX, :].reshape(HID, BX, TILE).astype(BF16)
        save(0, b).start()
        save(2, b).start()
        return carry

    lax.fori_loop(0, NB, low_block, 0)

    def top_block(b, carry):
        load(4, b).wait()
        cells = ctv.at[b].reshape(HID * BX, TILE)
        for i in range(0, BX, 2):
            x = b * BX + i
            cell = jnp.concatenate([cells[pl.ds(i + j, HID, stride=BX), :] for j in range(2)], axis=1)
            hidden, cell = update(windows(s_top, x, x + 1, 9 * CT, wte), cell)
            for j in range(2):
                part = slice(j * TILE, (j + 1) * TILE)
                cells[pl.ds(i + j, HID, stride=BX), :] = cell[:, part]
                tmp[pl.ds(i + j, HID, stride=BX), :] = hidden[:, part]
        htv[b] = tmp[0:HID * BX, :].reshape(HID, BX, TILE).astype(BF16)
        save(1, b).start()
        save(3, b).start()
        return carry

    lax.fori_loop(0, NB, top_block, 0)
    for k in range(4):
        for b in range(NB):
            save(k, b).wait()


def layers(fr, hl, cl, ht, ct, wl, bl, wt, bt, halos):
    anywhere = pl.BlockSpec(memory_space=pl.ANY)
    whole = pl.BlockSpec(memory_space=pltpu.VMEM)
    field = (HID, TILE, TILE)
    return pl.pallas_call(
        layers_kernel,
        out_shape=(
            jax.ShapeDtypeStruct(field, BF16),
            jax.ShapeDtypeStruct(field, BF16),
            jax.ShapeDtypeStruct(field, F32),
            jax.ShapeDtypeStruct(field, F32),
        ),
        in_specs=[anywhere] * 5 + [whole] * 9,
        out_specs=(anywhere,) * 4,
        scratch_shapes=[
            pltpu.VMEM((NB, CIN, BX, TILE), BF16),
            pltpu.VMEM((NB, HID, BX, TILE), BF16),
            pltpu.VMEM((NB, HID, BX, TILE), BF16),
            pltpu.VMEM((NB, HID, BX, TILE), F32),
            pltpu.VMEM((NB, HID, BX, TILE), F32),
            pltpu.VMEM((TILE + 4, 3 * CL, TILE), BF16),
            pltpu.VMEM((TILE + 2, 3 * CT, TILE), BF16),
            pltpu.VMEM((9 * CL, 3 * TILE), BF16),
            pltpu.VMEM((2, HID, 3 * TILE), F32),
            pltpu.VMEM((2, CL, TILE), F32),
            pltpu.VMEM((2, CT, TILE), F32),
            pltpu.VMEM((4 * HID, 9 * CL + 48), BF16),
            pltpu.VMEM((4 * HID, 9 * CT + TILE), BF16),
            pltpu.VMEM(((CL + HID) * BX, TILE), F32),
            pltpu.SemaphoreType.DMA((5, NB)),
            pltpu.SemaphoreType.DMA((4, NB)),
        ],
        compiler_params=pltpu.CompilerParams(vmem_limit_bytes=56 * 1024 * 1024),
        name="two_layers",
    )(fr, hl, cl, ht, ct, wl, bl, wt, bt, *halos)


def body(frames, hidden_low, cell_low, hidden_top, cell_top, weight_low, bias_low, weight_top, bias_top):
    fr = frames.reshape(frames.shape[2:])
    hl, cl, ht, ct = (field.reshape(field.shape[1:]) for field in (hidden_low, cell_low, hidden_top, cell_top))
    halos = exchange(fr, hl, ht, cl)
    th, ho, co, cto = layers(
        fr, hl, cl, ht, ct, weight_low.T, bias_low.reshape(1, -1), weight_top, bias_top.reshape(1, -1), halos
    )
    return th[None, None], ho[None], co[None], cto[None]


def solution(mesh):
    field = P(None, None, "lon", "lat")
    frame = P(None, None, None, "lon", "lat")
    return jax.shard_map(
        body,
        mesh=mesh,
        in_specs=(frame, field, field, field, field, P(), P(), P(), P()),
        out_specs=(frame, field, field, field),
        check_vma=False,
    )
```

```python
import functools

import jax
import jax.numpy as jnp
from jax import lax
from jax.experimental import pallas as pl
from jax.experimental.pallas import tpu as pltpu
from jax.sharding import PartitionSpec as P

CIN, HID, TILE, BX = 16, 64, 128, 16
CL = CIN + HID
CT = 2 * HID
NB = TILE // BX
PK = 2 * CL + HID
PA = CL + HID
F32, BF16 = jnp.float32, jnp.bfloat16
MESH = pl.DeviceIdType.MESH


def rot(block, shift):
    return pltpu.roll(block, shift % block.shape[1] if isinstance(shift, int) else shift, 1)


def lanes(shape):
    return lax.broadcasted_iota(jnp.int32, shape, 1)


def update(gates, cell):
    take = jnp.tanh(gates[0:HID])
    keep = jnp.tanh(gates[HID:2 * HID])
    cand = jnp.tanh(gates[2 * HID:3 * HID])
    show = jnp.tanh(gates[3 * HID:4 * HID])
    cell = 0.5 * ((keep + 1.0) * cell + (take + 1.0) * cand)
    return 0.5 * (show + 1.0) * jnp.tanh(cell), cell


def extended_weights(out, weight, bias, width):
    gate = lax.broadcasted_iota(jnp.int32, (4 * HID, 1), 0)
    half = jnp.where((gate >= 2 * HID) & (gate < 3 * HID), 1.0, 0.5)
    out[:, 0:width] = (weight * half).astype(BF16)
    spread = jnp.transpose(jnp.broadcast_to(bias, (TILE, 4 * HID))) * half
    high = spread.astype(BF16).astype(F32)
    mid = (spread - high).astype(BF16).astype(F32)
    low = spread - high - mid
    lane = lanes((4 * HID, TILE))
    tail = jnp.where(lane == 0, high, jnp.where(lane == 1, mid, jnp.where(lane == 2, low, 0.0)))
    out[:, width:width + 16] = tail[:, 0:16].astype(BF16)


def shifted(dest, at, base, width, stride, value, lane_lo, lane_hi):
    lane = lanes(value.shape)
    down = jnp.where(lane == 0, lane_lo, rot(value, 1))
    up = jnp.where(lane == TILE - 1, lane_hi, rot(value, TILE - 1))
    dest[at, base:base + width] = down.astype(BF16)
    dest[at, 2 * stride + base:2 * stride + base + width] = up.astype(BF16)


def interleaved(low, high):
    even = lax.rem(lanes(low.shape), 2) == 0
    high = rot(high, TILE - 1)
    return jnp.where(even, low, high), jnp.where(even, high, low)


def windows(source, first, second, width, weights):
    pair = jnp.concatenate(
        [source[pl.ds(first, 3)].reshape(width, TILE), source[pl.ds(second, 3)].reshape(width, TILE)], axis=1
    )
    ones = jnp.ones((16, 2 * TILE), BF16)
    return jnp.dot(weights[:, 0:width + 16], jnp.concatenate([pair, ones], axis=0), preferred_element_type=F32)


def lower_kernel(
    fr, hl, ht, cl, wl, bl,
    t_hid, t_ht, co, g_top, sp,
    frv, hlv, htv, clv, s_low, hid, strip, hs, g_low, wle, tmp,
    near_out, rest_out, cell_out, cor_out, lonb_out, lonf_out,
    near_in, rest_in, cell_in, cor_in, lonb_in, lonf_in,
    sem_in, sem_out, send_lat, recv_lat, send_cor, recv_cor, send_lon, recv_lon,
):
    nlon, nlat = lax.axis_size("lon"), lax.axis_size("lat")
    lon, lat = lax.axis_index("lon"), lax.axis_index("lat")
    loads = [
        pltpu.make_async_copy(src, dst, sem_in.at[k])
        for k, (src, dst) in enumerate(((fr, frv), (hl, hlv), (ht, htv)))
    ] + [
        pltpu.make_async_copy(cl.at[:, b * BX:(b + 1) * BX, :], clv.at[b], sem_in.at[3 + b]) for b in range(NB)
    ]
    for load in loads[0:2]:
        load.start()

    polars = [lat == 0, lat == nlat - 1]
    lat_targets, slots = [], []
    for side in range(2):
        to_lat = jnp.where(polars[side], lat, lat + (-1 if side == 0 else 1))
        shift = jnp.where(polars[side], nlon // 2, 0)
        slots.append(jnp.where(polars[side], side, 1 - side))
        lat_targets.append([(lax.rem(lon + shift + step + nlon, nlon), to_lat) for step in (-1, 0, 1)])
    lon_targets = [(lax.rem(lon + step + nlon, nlon), lat) for step in (-1, 1)]

    barrier = pltpu.get_barrier_semaphore()
    for target in lat_targets[0] + lat_targets[1] + lon_targets:
        pl.semaphore_signal(barrier, inc=1, device_id=target, device_id_type=MESH)

    row = lax.broadcasted_iota(jnp.int32, (16, TILE), 0)
    col = lax.broadcasted_iota(jnp.int32, (16, TILE), 1)
    wanted = jnp.where(row == 1, 1, jnp.where(row == 2, TILE - 1, jnp.where(row == 3, TILE - 2, 0)))
    pick = jnp.where((col == wanted) & (row < 4), 1.0, 0.0).astype(BF16)

    def columns(field, base, count):
        def step(k, carry):
            at = pl.multiple_of(k * 8, 8)
            found = lax.dot_general(
                pick, field[pl.ds(at, 8)].reshape(8 * TILE, TILE), (((1,), (1,)), ((), ())),
                preferred_element_type=F32,
            )
            for j in range(8):
                tmp[pl.ds(pl.multiple_of((base + at + j) * 8, 8), 8), :] = found[0:8, j * TILE:(j + 1) * TILE]
            return carry
        lax.fori_loop(0, count // 8, step, 0)

    def rows(field, count, base, whole):
        for side in range(2):
            start = 0 if side == 0 else TILE - BX
            tmp[0:count * BX, :] = field[:, start:start + BX, :].astype(F32).reshape(count * BX, TILE)
            first, second = (0, 1) if side == 0 else (BX - 1, BX - 2)
            lonb_out[side, base:base + count] = tmp[pl.ds(first, count, stride=BX), :].astype(BF16)
            if whole:
                lonb_out[side, CL + base:CL + base + count] = tmp[pl.ds(second, count, stride=BX), :].astype(BF16)

    copies = []

    def send(src, dst, send_sem, recv_sem, target):
        copies.append(pltpu.make_async_remote_copy(
            src_ref=src, dst_ref=dst, send_sem=send_sem, recv_sem=recv_sem,
            device_id=target, device_id_type=MESH))
        copies[-1].start()

    def received(src, dst, send_sem, recv_sem):
        pltpu.make_async_remote_copy(
            src_ref=src, dst_ref=dst, send_sem=send_sem, recv_sem=recv_sem,
            device_id=lon_targets[0], device_id_type=MESH).wait_recv()

    for load in loads[0:2]:
        load.wait()
    for load in loads[2:]:
        load.start()
    columns(frv, 0, CIN)
    columns(hlv, CIN, HID)
    for side in range(2):
        near_out[side] = tmp[pl.ds(2 * side, CL, stride=8), :].astype(BF16)
        rest_out[side, 0:CL] = tmp[pl.ds(2 * side + 1, CL, stride=8), :].astype(BF16)
    pl.semaphore_wait(barrier, 8)
    for side in range(2):
        send(near_out.at[side], near_in.at[slots[side]], send_lat.at[0, side], recv_lat.at[0, slots[side]],
             lat_targets[side][1])

    rows(frv, CIN, 0, True)
    rows(hlv, HID, CIN, True)
    loads[2].wait()
    rows(htv, HID, 2 * CL, False)
    for side in range(2):
        send(lonb_out.at[side], lonb_in.at[1 - side], send_lon.at[0, side], recv_lon.at[0, 1 - side],
             lon_targets[side])
    columns(htv, 0, HID)
    for side in range(2):
        rest_out[side, CL:PA] = tmp[pl.ds(2 * side, HID, stride=8), :].astype(BF16)
        send(rest_out.at[side], rest_in.at[slots[side]], send_lat.at[1, side], recv_lat.at[1, slots[side]],
             lat_targets[side][1])

    for load in loads[3:]:
        load.wait()

    def cell_columns(k, carry):
        for j in range(4):
            turned = jnp.transpose(jnp.concatenate([clv[b, k * 4 + j] for b in range(NB)], axis=0))
            at = pl.multiple_of((k * 4 + j) * 8, 8)
            tmp[pl.ds(at, 8), :] = jnp.where(
                lax.broadcasted_iota(jnp.int32, (8, TILE), 0) < 4, turned[0:8], turned[TILE - 8:TILE])
        return carry

    lax.fori_loop(0, HID // 4, cell_columns, 0)
    for side in range(2):
        cell_out[side] = tmp[pl.ds(7 * side, HID, stride=8), :]
    for side in range(2):
        block, first = (0, 0) if side == 0 else (NB - 1, BX - 1)
        lonf_out[side] = clv.at[block].reshape(HID * BX, TILE)[pl.ds(first, HID, stride=BX), :]

    for side in range(2):
        near = near_out[side].astype(F32)
        rest = rest_out[side].astype(F32)
        cell = cell_out[side]
        high = cell.astype(BF16).astype(F32)
        mid = (cell - high).astype(BF16).astype(F32)
        low = cell - high - mid
        pad = jnp.zeros((CL - HID, TILE), F32)
        wide = [near, near, rest[0:CL], rest[0:CL]] + [
            jnp.concatenate([part, pad], axis=0) for part in (rest[CL:PA], high, mid, low)]
        for step in range(2):
            ends = (0, 1) if step == 0 else (TILE - 1, TILE - 2)
            source = (ends[0], ends[1], ends[0], ends[1], ends[0], ends[0], ends[0], ends[0])
            lane = lanes((CL, TILE))
            package = jnp.zeros((CL, TILE), F32)
            for k in range(8):
                package = jnp.where(lane == k, rot(wide[k], k - source[k] + TILE), package)
            cor_out[side, step] = package.astype(BF16)
    for side in range(2):
        for step in range(2):
            send(cor_out.at[side, step], cor_in.at[slots[side], 1 - step], send_cor.at[side, step],
                 recv_cor.at[slots[side], 1 - step], lat_targets[side][2 * step])
    for side in range(2):
        send(cell_out.at[side], cell_in.at[slots[side]], send_lat.at[2, side], recv_lat.at[2, slots[side]],
             lat_targets[side][1])
        send(lonf_out.at[side], lonf_in.at[1 - side], send_lon.at[1, side], recv_lon.at[1, 1 - side],
             lon_targets[side])

    def relayout(b, carry):
        at = pl.multiple_of(b * BX, BX)
        s_low[pl.ds(at + 2, BX), CL:CL + CIN] = jnp.swapaxes(frv[:, pl.ds(at, BX), :], 0, 1)
        s_low[pl.ds(at + 2, BX), CL + CIN:2 * CL] = jnp.swapaxes(hlv[:, pl.ds(at, BX), :], 0, 1)
        hid[1, pl.ds(at, BX)] = jnp.swapaxes(htv[:, pl.ds(at, BX), :], 0, 1)
        return carry

    lax.fori_loop(0, NB, relayout, 0)
    saves = [pltpu.make_async_copy(hid.at[1], t_ht, sem_out.at[0, 0])]
    saves[0].start()
    extended_weights(wle, jnp.transpose(wl[...].astype(F32)), bl[...], 9 * CL)

    for slot in range(2):
        received(near_out.at[0], near_in.at[slot], send_lat.at[0, slot], recv_lat.at[0, slot])
    for k, tile in enumerate(interleaved(near_in[0].astype(F32), near_in[1].astype(F32))):
        g_low[k] = tile.astype(BF16)

    def shift_row(x, parity):
        halo = rot(g_low[parity].astype(F32), lax.rem(TILE - x, TILE))
        shifted(s_low, x + 2, 0, CL, CL, s_low[x + 2, CL:2 * CL].astype(F32), halo, halo)

    def shift_first(i, carry):
        for j in range(4):
            shift_row(BX + 4 * i + j, j % 2)
        return carry

    shift_row(BX - 1, 1)
    lax.fori_loop(0, BX // 4, shift_first, 0)

    def low_rows(b, i):
        x = b * BX + i
        ahead = lax.rem(b + 1, NB) * BX + i
        cells = clv.at[b].reshape(HID * BX, TILE)
        cell = jnp.concatenate([cells[pl.ds(i + j, HID, stride=BX), :] for j in range(2)], axis=1)
        hidden, cell = update(windows(s_low, x + 1, x + 2, 9 * CL, wle), cell)
        for j in range(2):
            shift_row(ahead + j, j)
            part = slice(j * TILE, (j + 1) * TILE)
            cells[pl.ds(i + j, HID, stride=BX), :] = cell[:, part]
            hid[0, x + j] = hidden[:, part].astype(BF16)

    def save_block(b):
        at = pl.multiple_of(b * BX, BX)
        return (
            pltpu.make_async_copy(clv.at[b], co.at[b], sem_out.at[1, b]),
            pltpu.make_async_copy(hid.at[0, pl.ds(at, BX)], t_hid.at[pl.ds(at, BX)], sem_out.at[2, b]),
        )

    def low_block(k, carry):
        b = lax.rem(k, NB)
        for i in range(0, BX, 2):
            low_rows(b, i)
        for save in save_block(b):
            save.start()
        return carry

    lax.fori_loop(1, NB - 1, low_block, 0)

    for slot in range(2):
        received(lonb_out.at[0], lonb_in.at[slot], send_lon.at[0, slot], recv_lon.at[0, slot])
        for step in range(2):
            received(cor_out.at[0, 0], cor_in.at[slot, step], send_cor.at[slot, step], recv_cor.at[slot, step])

    for at, side, far in ((1, 0, 0), (0, 0, 1), (130, 1, 0), (131, 1, 1)):
        value = lonb_in[side, far * CL:far * CL + CL].astype(F32)
        lo = rot(cor_in[0, side].astype(F32), TILE - far)
        hi = rot(cor_in[1, side].astype(F32), TILE - 1 - far)
        s_low[at, CL:2 * CL] = value.astype(BF16)
        shifted(s_low, at, 0, CL, CL, value, lo, hi)
    lax.fori_loop(NB - 1, NB + 1, low_block, 0)

    for slot in range(2):
        received(rest_out.at[0], rest_in.at[slot], send_lat.at[1, slot], recv_lat.at[1, slot])
        received(cell_out.at[0], cell_in.at[slot], send_lat.at[2, slot], recv_lat.at[2, slot])
        received(lonf_out.at[0], lonf_in.at[slot], send_lon.at[1, slot], recv_lon.at[1, slot])
    for side in range(2):
        lane = lanes((CL, TILE))
        west = cor_in[side, 0].astype(F32)
        east = cor_in[side, 1].astype(F32)
        near = jnp.concatenate([
            jnp.where(lane == TILE - 1, rot(west, TILE - 1), rot(west, TILE - 3)),
            near_in[side].astype(F32), east], axis=1)
        far = jnp.concatenate([
            jnp.where(lane == TILE - 1, rot(west, TILE - 3), rot(west, TILE - 5)),
            rest_in[side, 0:CL].astype(F32), rot(east, TILE - 2)], axis=1)
        edge = 0 if side == 0 else TILE - 1
        parts = [lonb_in[0, 0:CL], lonb_in[0, CL:2 * CL], lonb_in[1, 0:CL], lonb_in[1, CL:2 * CL]]
        parts = [part.astype(F32) for part in parts]
        mine = jnp.concatenate([
            jnp.where(lane == TILE - 1, rot(parts[0], TILE - 1 - edge), rot(parts[1], 2 * TILE - 2 - edge)),
            near_out[side].astype(F32),
            jnp.where(lane == 0, rot(parts[2], TILE - edge), rot(parts[3], TILE + 1 - edge))], axis=1)
        outer = jnp.where(polars[side], mine, far)
        inner = jnp.where(polars[side], far, mine)
        order = (outer, near, inner) if side == 0 else (inner, near, outer)
        for e in range(3):
            for a in range(3):
                at = (3 * a + e) * CL
                strip[at:at + CL, :] = rot(order[e], 1 - a).astype(BF16)
        gates = jnp.dot(
            wle[:, 0:9 * CL + 16],
            jnp.concatenate([strip[...], jnp.ones((16, 3 * TILE), BF16)], axis=0),
            preferred_element_type=F32,
        )
        west, east = west[0:HID], east[0:HID]
        cell = jnp.concatenate([
            rot(west, TILE - 6) + rot(west, TILE - 7) + rot(west, TILE - 8),
            cell_in[side],
            rot(east, TILE - 5) + rot(east, TILE - 6) + rot(east, TILE - 7)], axis=1)
        hs[side], _ = update(gates, cell)

    for k, tile in enumerate(interleaved(hs[0, :, TILE:2 * TILE], hs[1, :, TILE:2 * TILE])):
        g_top[k, 0:HID] = tile.astype(BF16)
    for k, tile in enumerate(interleaved(rest_in[0, CL:PA].astype(F32), rest_in[1, CL:PA].astype(F32))):
        g_top[k, HID:CT] = tile.astype(BF16)

    hidden, _ = update(windows(s_low, 0, 129, 9 * CL, wle), jnp.concatenate([lonf_in[0], lonf_in[1]], axis=1))
    for side in range(2):
        src = TILE - 1 if side == 0 else 0
        value = hidden[:, side * TILE:(side + 1) * TILE]
        lo = rot(hs[0, :, 2 * side * TILE:(2 * side + 1) * TILE], TILE - src)
        hi = rot(hs[1, :, 2 * side * TILE:(2 * side + 1) * TILE], 2 * TILE - 1 - src)
        sp[side, CT:CT + HID] = value.astype(BF16)
        shifted(sp, side, 0, HID, CT, value, lo, hi)
        value = lonb_in[side, 2 * CL:PK].astype(F32)
        lo = rot(cor_in[0, side, 0:HID].astype(F32), TILE - 4)
        hi = rot(cor_in[1, side, 0:HID].astype(F32), TILE - 5)
        sp[side, CT + HID:2 * CT] = value.astype(BF16)
        shifted(sp, side, HID, HID, CT, value, lo, hi)

    for copy in copies:
        copy.wait_send()
    for b in range(NB):
        for save in save_block(b):
            save.wait()
    saves[0].wait()


def lower_layer(fr, hl, ht, cl, wl, bl):
    anywhere = pl.BlockSpec(memory_space=pl.ANY)
    whole = pl.BlockSpec(memory_space=pltpu.VMEM)
    exchanged = [
        pltpu.VMEM((2, CL, TILE), BF16),
        pltpu.VMEM((2, PA, TILE), BF16),
        pltpu.VMEM((2, HID, TILE), F32),
        pltpu.VMEM((2, 2, CL, TILE), BF16),
        pltpu.VMEM((2, PK, TILE), BF16),
        pltpu.VMEM((2, HID, TILE), F32),
    ]
    return pl.pallas_call(
        lower_kernel,
        out_shape=(
            jax.ShapeDtypeStruct((TILE, HID, TILE), BF16),
            jax.ShapeDtypeStruct((TILE, HID, TILE), BF16),
            jax.ShapeDtypeStruct((NB, HID, BX, TILE), F32),
            jax.ShapeDtypeStruct((2, CT, TILE), BF16),
            jax.ShapeDtypeStruct((2, 3 * CT, TILE), BF16),
        ),
        in_specs=[anywhere] * 4 + [whole] * 2,
        out_specs=(anywhere, anywhere, anywhere, whole, whole),
        scratch_shapes=[
            pltpu.VMEM((CIN, TILE, TILE), BF16),
            pltpu.VMEM((HID, TILE, TILE), BF16),
            pltpu.VMEM((HID, TILE, TILE), BF16),
            pltpu.VMEM((NB, HID, BX, TILE), F32),
            pltpu.VMEM((TILE + 4, 3 * CL, TILE), BF16),
            pltpu.VMEM((2, TILE, HID, TILE), BF16),
            pltpu.VMEM((9 * CL, 3 * TILE), BF16),
            pltpu.VMEM((2, HID, 3 * TILE), F32),
            pltpu.VMEM((2, CL, TILE), BF16),
            pltpu.VMEM((4 * HID, 9 * CL + 48), BF16),
            pltpu.VMEM((HID * BX, TILE), F32),
            *exchanged,
            *exchanged,
            pltpu.SemaphoreType.DMA((3 + NB,)),
            pltpu.SemaphoreType.DMA((3, NB)),
            pltpu.SemaphoreType.DMA((3, 2)),
            pltpu.SemaphoreType.DMA((3, 2)),
            pltpu.SemaphoreType.DMA((2, 2)),
            pltpu.SemaphoreType.DMA((2, 2)),
            pltpu.SemaphoreType.DMA((2, 2)),
            pltpu.SemaphoreType.DMA((2, 2)),
        ],
        compiler_params=pltpu.CompilerParams(
            collective_id=0, has_side_effects=True, vmem_limit_bytes=60 * 1024 * 1024
        ),
        name="lower_layer",
    )(fr, hl, ht, cl, wl, bl)


def upper_kernel(
    t_hid, t_ht, co_in, ct, g_top, sp, wt, bt,
    th, ho, co, cto,
    ctv, cov, hov, thv, s_top, wte, rows,
    sem_in, sem_out,
):
    def span(b):
        return pl.ds(pl.multiple_of(b * BX, BX), BX)

    def load(k, b):
        if k >= 2:
            source, dest = (ct.at[:, span(b), :], ctv.at[b]) if k == 2 else (co_in.at[b], cov.at[b])
            return pltpu.make_async_copy(source, dest, sem_in.at[k, b])
        source = (t_hid, t_ht)[k]
        at = CT + k * HID
        return pltpu.make_async_copy(
            source.at[span(b)], s_top.at[pl.ds(b * BX + 1, BX), at:at + HID, :], sem_in.at[k, b])

    def save(k, b):
        source, dest = ((hov, ho), (thv, th), (ctv, cto), (cov, co))[k]
        return pltpu.make_async_copy(source.at[b], dest.at[:, span(b), :], sem_out.at[k, b])

    for b in range(2):
        for k in range(4):
            load(k, b).start()

    extended_weights(wte, wt[...].astype(F32), bt[...], 9 * CT)
    s_top[0] = sp[0]
    s_top[TILE + 1] = sp[1]

    def shift_row(x, parity):
        halo = rot(g_top[parity].astype(F32), lax.rem(TILE - x, TILE))
        shifted(s_top, x + 1, 0, CT, CT, s_top[x + 1, CT:2 * CT].astype(F32), halo, halo)

    for k in range(2):
        load(k, 0).wait()

    def shift_first(i, carry):
        for j in range(4):
            shift_row(4 * i + j, j % 2)
        return carry

    lax.fori_loop(0, BX // 4, shift_first, 0)

    def top_rows(b, i, shift):
        x = b * BX + i
        cells = ctv.at[b].reshape(HID * BX, TILE)
        cell = jnp.concatenate([cells[pl.ds(i + j, HID, stride=BX), :] for j in range(2)], axis=1)
        hidden, cell = update(windows(s_top, x, x + 1, 9 * CT, wte), cell)
        for j in range(2):
            if shift:
                shift_row(x + BX + j, j)
            part = slice(j * TILE, (j + 1) * TILE)
            cells[pl.ds(i + j, HID, stride=BX), :] = cell[:, part]
            rows[i + j] = hidden[:, part].astype(BF16)

    def top_block(b, shift):
        @pl.when(b + 2 < NB)
        def _():
            for k in range(4):
                load(k, b + 2).start()

        load(2, b).wait()
        if shift:
            for k in range(2):
                load(k, b + 1).wait()
        load(3, b).wait()
        hov[b] = jnp.swapaxes(s_top[pl.ds(b * BX + 1, BX), CT:CT + HID], 0, 1)
        before = jnp.maximum(b - 1, 0)
        thv[before] = jnp.swapaxes(rows[...], 0, 1)
        for i in range(0, BX, 2):
            top_rows(b, i, shift)
        for k in (0, 2, 3):
            save(k, b).start()

        @pl.when(b > 0)
        def _():
            save(1, before).start()

    def top_step(b, carry):
        top_block(b, True)
        return carry

    rows[...] = jnp.zeros(rows.shape, BF16)
    lax.fori_loop(0, NB - 1, top_step, 0)
    top_block(NB - 1, False)
    thv[NB - 1] = jnp.swapaxes(rows[...], 0, 1)
    save(1, NB - 1).start()
    for k in range(4):
        for b in range(NB):
            save(k, b).wait()


def upper_layer(t_hid, t_ht, co, ct, g_top, sp, wt, bt):
    anywhere = pl.BlockSpec(memory_space=pl.ANY)
    whole = pl.BlockSpec(memory_space=pltpu.VMEM)
    field = (HID, TILE, TILE)
    return pl.pallas_call(
        upper_kernel,
        out_shape=(
            jax.ShapeDtypeStruct(field, BF16),
            jax.ShapeDtypeStruct(field, BF16),
            jax.ShapeDtypeStruct(field, F32),
            jax.ShapeDtypeStruct(field, F32),
        ),
        in_specs=[anywhere] * 4 + [whole] * 4,
        out_specs=(anywhere,) * 4,
        scratch_shapes=[
            pltpu.VMEM((NB, HID, BX, TILE), F32),
            pltpu.VMEM((NB, HID, BX, TILE), F32),
            pltpu.VMEM((NB, HID, BX, TILE), BF16),
            pltpu.VMEM((NB, HID, BX, TILE), BF16),
            pltpu.VMEM((TILE + 2, 3 * CT, TILE), BF16),
            pltpu.VMEM((4 * HID, 9 * CT + TILE), BF16),
            pltpu.VMEM((BX, HID, TILE), BF16),
            pltpu.SemaphoreType.DMA((4, NB)),
            pltpu.SemaphoreType.DMA((4, NB)),
        ],
        compiler_params=pltpu.CompilerParams(vmem_limit_bytes=60 * 1024 * 1024),
        name="upper_layer",
    )(t_hid, t_ht, co, ct, g_top, sp, wt, bt)


def body(frames, hidden_low, cell_low, hidden_top, cell_top, weight_low, bias_low, weight_top, bias_top):
    fr = frames.reshape(frames.shape[2:])
    hl, cl, ht, ct = (field.reshape(field.shape[1:]) for field in (hidden_low, cell_low, hidden_top, cell_top))
    t_hid, t_ht, co, g_top, sp = lower_layer(fr, hl, ht, cl, weight_low.T, bias_low.reshape(1, -1))
    th, ho, co, cto = upper_layer(t_hid, t_ht, co, ct, g_top, sp, weight_top, bias_top.reshape(1, -1))
    return th[None, None], ho[None], co[None], cto[None]


def solution(mesh):
    field = P(None, None, "lon", "lat")
    frame = P(None, None, None, "lon", "lat")
    return jax.shard_map(
        body,
        mesh=mesh,
        in_specs=(frame, field, field, field, field, P(), P(), P(), P()),
        out_specs=(frame, field, field, field),
        check_vma=False,
    )
```

```python
import functools

import jax
import jax.numpy as jnp
from jax import lax
from jax.experimental import pallas as pl
from jax.experimental.pallas import tpu as pltpu
from jax.sharding import PartitionSpec as P

CIN, HID, TILE, BX = 16, 64, 128, 16
CL = CIN + HID
CT = 2 * HID
NB = TILE // BX
PITCH = 24
PK = 2 * CL + HID
PA = CL + HID
F32, BF16 = jnp.float32, jnp.bfloat16
MESH = pl.DeviceIdType.MESH


def rot(block, shift):
    return pltpu.roll(block, shift % block.shape[1] if isinstance(shift, int) else shift, 1)


def lanes(shape):
    return lax.broadcasted_iota(jnp.int32, shape, 1)


def update(gates, cell):
    take = jnp.tanh(gates[0:HID])
    keep = jnp.tanh(gates[HID:2 * HID])
    cand = jnp.tanh(gates[2 * HID:3 * HID])
    show = jnp.tanh(gates[3 * HID:4 * HID])
    cell = 0.5 * ((keep + 1.0) * cell + (take + 1.0) * cand)
    return 0.5 * (show + 1.0) * jnp.tanh(cell), cell


def extended_weights(out, weight, bias, width):
    gate = lax.broadcasted_iota(jnp.int32, (4 * HID, 1), 0)
    half = jnp.where((gate >= 2 * HID) & (gate < 3 * HID), 1.0, 0.5)
    out[:, 0:width] = (weight * half).astype(BF16)
    spread = jnp.transpose(jnp.broadcast_to(bias, (TILE, 4 * HID))) * half
    high = spread.astype(BF16).astype(F32)
    mid = (spread - high).astype(BF16).astype(F32)
    low = spread - high - mid
    lane = lanes((4 * HID, TILE))
    tail = jnp.where(lane == 0, high, jnp.where(lane == 1, mid, jnp.where(lane == 2, low, 0.0)))
    out[:, width:width + 16] = tail[:, 0:16].astype(BF16)


def shifted(dest, at, base, width, stride, value, lane_lo, lane_hi):
    lane = lanes(value.shape)
    down = jnp.where(lane == 0, lane_lo, rot(value, 1))
    up = jnp.where(lane == TILE - 1, lane_hi, rot(value, TILE - 1))
    dest[at, base:base + width] = down.astype(BF16)
    dest[at, 2 * stride + base:2 * stride + base + width] = up.astype(BF16)


def interleaved(low, high):
    even = lax.rem(lanes(low.shape), 2) == 0
    high = rot(high, TILE - 1)
    return jnp.where(even, low, high), jnp.where(even, high, low)


def windows(source, first, second, width, weights):
    pair = jnp.concatenate(
        [source[pl.ds(first, 3)].reshape(width, TILE), source[pl.ds(second, 3)].reshape(width, TILE)], axis=1
    )
    ones = jnp.ones((16, 2 * TILE), BF16)
    return jnp.dot(weights[:, 0:width + 16], jnp.concatenate([pair, ones], axis=0), preferred_element_type=F32)


def lower_kernel(
    fr, hl, ht, cl, wl, bl,
    t_hid, t_ht, co, g_top, sp,
    frv, hlv, htv, clv, s_low, hid, strip, hs, g_low, wle, tmp, ctmp,
    near_out, rest_out, cell_out, cor_out, lonb_out, lonf_out,
    near_in, rest_in, cell_in, cor_in, lonb_in, lonf_in,
    sem_in, sem_out, send_lat, recv_lat, send_cor, recv_cor, send_lon, recv_lon,
):
    nlon, nlat = lax.axis_size("lon"), lax.axis_size("lat")
    lon, lat = lax.axis_index("lon"), lax.axis_index("lat")
    loads = [
        pltpu.make_async_copy(src, dst, sem_in.at[k])
        for k, (src, dst) in enumerate(((fr, frv), (hl, hlv), (ht, htv)))
    ] + [
        pltpu.make_async_copy(cl.at[:, b * BX:(b + 1) * BX, :], clv.at[b, :, 0:BX, :], sem_in.at[3 + b]) for b in range(NB)
    ]
    for load in loads[0:2]:
        load.start()

    polars = [lat == 0, lat == nlat - 1]
    lat_targets, slots = [], []
    for side in range(2):
        to_lat = jnp.where(polars[side], lat, lat + (-1 if side == 0 else 1))
        shift = jnp.where(polars[side], nlon // 2, 0)
        slots.append(jnp.where(polars[side], side, 1 - side))
        lat_targets.append([(lax.rem(lon + shift + step + nlon, nlon), to_lat) for step in (-1, 0, 1)])
    lon_targets = [(lax.rem(lon + step + nlon, nlon), lat) for step in (-1, 1)]

    barrier = pltpu.get_barrier_semaphore()
    for target in lat_targets[0] + lat_targets[1] + lon_targets:
        pl.semaphore_signal(barrier, inc=1, device_id=target, device_id_type=MESH)

    row = lax.broadcasted_iota(jnp.int32, (16, TILE), 0)
    col = lax.broadcasted_iota(jnp.int32, (16, TILE), 1)
    wanted = jnp.where(row == 1, 1, jnp.where(row == 2, TILE - 1, jnp.where(row == 3, TILE - 2, 0)))
    pick = jnp.where((col == wanted) & (row < 4), 1.0, 0.0).astype(BF16)

    def columns(field, base, k):
        at = pl.multiple_of(k * 8, 8)
        found = lax.dot_general(
            pick, field[pl.ds(at, 8)].reshape(8 * TILE, TILE), (((1,), (1,)), ((), ())),
            preferred_element_type=F32,
        )
        for j in range(8):
            tmp[pl.ds(pl.multiple_of((base + at + j) * 8, 8), 8), :] = found[0:8, j * TILE:(j + 1) * TILE]

    def rows(field, count, base, whole):
        for side in range(2):
            start = 0 if side == 0 else TILE - BX
            tmp[0:count * BX, :] = field[:, start:start + BX, :].astype(F32).reshape(count * BX, TILE)
            first, second = (0, 1) if side == 0 else (BX - 1, BX - 2)
            lonb_out[side, base:base + count] = tmp[pl.ds(first, count, stride=BX), :].astype(BF16)
            if whole:
                lonb_out[side, CL + base:CL + base + count] = tmp[pl.ds(second, count, stride=BX), :].astype(BF16)

    copies = []

    def send(src, dst, send_sem, recv_sem, target):
        copies.append(pltpu.make_async_remote_copy(
            src_ref=src, dst_ref=dst, send_sem=send_sem, recv_sem=recv_sem,
            device_id=target, device_id_type=MESH))
        copies[-1].start()

    def received(src, dst, send_sem, recv_sem):
        pltpu.make_async_remote_copy(
            src_ref=src, dst_ref=dst, send_sem=send_sem, recv_sem=recv_sem,
            device_id=lon_targets[0], device_id_type=MESH).wait_recv()

    for load in loads[0:2]:
        load.wait()
    for load in loads[2:]:
        load.start()
    for k in range(CIN // 8):
        columns(frv, 0, k)

    def hidden_columns(k, carry):
        columns(hlv, CIN, 2 * k)
        columns(hlv, CIN, 2 * k + 1)
        return carry

    lax.fori_loop(0, HID // 16, hidden_columns, 0)
    for side in range(2):
        near_out[side] = tmp[pl.ds(2 * side, CL, stride=8), :].astype(BF16)
        rest_out[side, 0:CL] = tmp[pl.ds(2 * side + 1, CL, stride=8), :].astype(BF16)
    pl.semaphore_wait(barrier, 8)
    for side in range(2):
        send(near_out.at[side], near_in.at[slots[side]], send_lat.at[0, side], recv_lat.at[0, slots[side]],
             lat_targets[side][1])

    rows(frv, CIN, 0, True)
    rows(hlv, HID, CIN, True)
    extended_weights(wle, jnp.transpose(wl[...].astype(F32)), bl[...], 9 * CL)
    loads[2].wait()
    rows(htv, HID, 2 * CL, False)
    for side in range(2):
        send(lonb_out.at[side], lonb_in.at[1 - side], send_lon.at[0, side], recv_lon.at[0, 1 - side],
             lon_targets[side])
    for load in loads[3:]:
        load.wait()

    def relayout(b, carry):
        at = pl.multiple_of(b * BX, BX)
        columns(htv, 0, b)
        for j in range(8):
            turned = jnp.transpose(jnp.concatenate([clv[k, b * 8 + j, 0:BX] for k in range(NB)], axis=0))
            ctmp[pl.ds(pl.multiple_of((b * 8 + j) * 8, 8), 8), :] = jnp.where(
                lax.broadcasted_iota(jnp.int32, (8, TILE), 0) < 4, turned[0:8], turned[TILE - 8:TILE])
        s_low[pl.ds(at + 2, BX), CL:CL + CIN] = jnp.swapaxes(frv[:, pl.ds(at, BX), :], 0, 1)
        s_low[pl.ds(at + 2, BX), CL + CIN:2 * CL] = jnp.swapaxes(hlv[:, pl.ds(at, BX), :], 0, 1)
        hid[1, pl.ds(at, BX)] = jnp.swapaxes(htv[:, pl.ds(at, BX), :], 0, 1)
        return carry

    lax.fori_loop(0, NB, relayout, 0)
    for side in range(2):
        rest_out[side, CL:PA] = tmp[pl.ds(2 * side, HID, stride=8), :].astype(BF16)
        send(rest_out.at[side], rest_in.at[slots[side]], send_lat.at[1, side], recv_lat.at[1, slots[side]],
             lat_targets[side][1])
        cell_out[side] = ctmp[pl.ds(7 * side, HID, stride=8), :]
    for side in range(2):
        block, first = (0, 0) if side == 0 else (NB - 1, BX - 1)
        lonf_out[side] = clv.at[block].reshape(HID * PITCH, TILE)[pl.ds(first, HID, stride=PITCH), :]

    for side in range(2):
        near = near_out[side].astype(F32)
        rest = rest_out[side].astype(F32)
        cell = cell_out[side]
        high = cell.astype(BF16).astype(F32)
        mid = (cell - high).astype(BF16).astype(F32)
        low = cell - high - mid
        pad = jnp.zeros((CL - HID, TILE), F32)
        wide = [near, near, rest[0:CL], rest[0:CL]] + [
            jnp.concatenate([part, pad], axis=0) for part in (rest[CL:PA], high, mid, low)]
        for step in range(2):
            ends = (0, 1) if step == 0 else (TILE - 1, TILE - 2)
            source = (ends[0], ends[1], ends[0], ends[1], ends[0], ends[0], ends[0], ends[0])
            lane = lanes((CL, TILE))
            package = jnp.zeros((CL, TILE), F32)
            for k in range(8):
                package = jnp.where(lane == k, rot(wide[k], k - source[k] + TILE), package)
            cor_out[side, step] = package.astype(BF16)
    for side in range(2):
        for step in range(2):
            send(cor_out.at[side, step], cor_in.at[slots[side], 1 - step], send_cor.at[side, step],
                 recv_cor.at[slots[side], 1 - step], lat_targets[side][2 * step])
    for side in range(2):
        send(cell_out.at[side], cell_in.at[slots[side]], send_lat.at[2, side], recv_lat.at[2, slots[side]],
             lat_targets[side][1])
        send(lonf_out.at[side], lonf_in.at[1 - side], send_lon.at[1, side], recv_lon.at[1, 1 - side],
             lon_targets[side])

    saves = [pltpu.make_async_copy(hid.at[1], t_ht, sem_out.at[0, 0])]
    saves[0].start()

    for slot in range(2):
        received(near_out.at[0], near_in.at[slot], send_lat.at[0, slot], recv_lat.at[0, slot])
    for k, tile in enumerate(interleaved(near_in[0].astype(F32), near_in[1].astype(F32))):
        g_low[k] = tile.astype(BF16)

    def shift_row(x, parity):
        halo = rot(g_low[parity].astype(F32), lax.rem(TILE - x, TILE))
        shifted(s_low, x + 2, 0, CL, CL, s_low[x + 2, CL:2 * CL].astype(F32), halo, halo)

    def shift_first(i, carry):
        for j in range(4):
            shift_row(BX + 4 * i + j, j % 2)
        return carry

    shift_row(BX - 1, 1)
    lax.fori_loop(0, BX // 4, shift_first, 0)

    def low_rows(b, i):
        x = b * BX + i
        ahead = lax.rem(b + 1, NB) * BX + i
        cells = clv.at[b].reshape(HID * PITCH, TILE)
        cell = jnp.concatenate([cells[pl.ds(i + j, HID, stride=PITCH), :] for j in range(2)], axis=1)
        hidden, cell = update(windows(s_low, x + 1, x + 2, 9 * CL, wle), cell)
        for j in range(2):
            shift_row(ahead + j, j)
            part = slice(j * TILE, (j + 1) * TILE)
            cells[pl.ds(i + j, HID, stride=PITCH), :] = cell[:, part]
            hid[0, x + j] = hidden[:, part].astype(BF16)

    def save_block(b):
        at = pl.multiple_of(b * BX, BX)
        return (
            pltpu.make_async_copy(clv.at[b, :, 0:BX, :], co.at[b], sem_out.at[1, b]),
            pltpu.make_async_copy(hid.at[0, pl.ds(at, BX)], t_hid.at[pl.ds(at, BX)], sem_out.at[2, b]),
        )

    def low_block(b):
        for i in range(0, BX, 2):
            low_rows(b, i)
        for save in save_block(b):
            save.start()

    def low_step(k, carry):
        low_block(2 * k + 1)
        low_block(2 * k + 2)
        return carry

    lax.fori_loop(0, NB // 2 - 1, low_step, 0)

    for slot in range(2):
        received(lonb_out.at[0], lonb_in.at[slot], send_lon.at[0, slot], recv_lon.at[0, slot])
        for step in range(2):
            received(cor_out.at[0, 0], cor_in.at[slot, step], send_cor.at[slot, step], recv_cor.at[slot, step])

    for at, side, far in ((1, 0, 0), (0, 0, 1), (130, 1, 0), (131, 1, 1)):
        value = lonb_in[side, far * CL:far * CL + CL].astype(F32)
        lo = rot(cor_in[0, side].astype(F32), TILE - far)
        hi = rot(cor_in[1, side].astype(F32), TILE - 1 - far)
        s_low[at, CL:2 * CL] = value.astype(BF16)
        shifted(s_low, at, 0, CL, CL, value, lo, hi)
    low_block(NB - 1)
    low_block(0)

    for slot in range(2):
        received(rest_out.at[0], rest_in.at[slot], send_lat.at[1, slot], recv_lat.at[1, slot])
        received(cell_out.at[0], cell_in.at[slot], send_lat.at[2, slot], recv_lat.at[2, slot])
        received(lonf_out.at[0], lonf_in.at[slot], send_lon.at[1, slot], recv_lon.at[1, slot])
    for side in range(2):
        lane = lanes((CL, TILE))
        west = cor_in[side, 0].astype(F32)
        east = cor_in[side, 1].astype(F32)
        near = jnp.concatenate([
            jnp.where(lane == TILE - 1, rot(west, TILE - 1), rot(west, TILE - 3)),
            near_in[side].astype(F32), east], axis=1)
        far = jnp.concatenate([
            jnp.where(lane == TILE - 1, rot(west, TILE - 3), rot(west, TILE - 5)),
            rest_in[side, 0:CL].astype(F32), rot(east, TILE - 2)], axis=1)
        edge = 0 if side == 0 else TILE - 1
        parts = [lonb_in[0, 0:CL], lonb_in[0, CL:2 * CL], lonb_in[1, 0:CL], lonb_in[1, CL:2 * CL]]
        parts = [part.astype(F32) for part in parts]
        mine = jnp.concatenate([
            jnp.where(lane == TILE - 1, rot(parts[0], TILE - 1 - edge), rot(parts[1], 2 * TILE - 2 - edge)),
            near_out[side].astype(F32),
            jnp.where(lane == 0, rot(parts[2], TILE - edge), rot(parts[3], TILE + 1 - edge))], axis=1)
        outer = jnp.where(polars[side], mine, far)
        inner = jnp.where(polars[side], far, mine)
        order = (outer, near, inner) if side == 0 else (inner, near, outer)
        for e in range(3):
            for a in range(3):
                at = (3 * a + e) * CL
                strip[at:at + CL, :] = rot(order[e], 1 - a).astype(BF16)
        gates = jnp.dot(
            wle[:, 0:9 * CL + 16],
            jnp.concatenate([strip[...], jnp.ones((16, 3 * TILE), BF16)], axis=0),
            preferred_element_type=F32,
        )
        west, east = west[0:HID], east[0:HID]
        cell = jnp.concatenate([
            rot(west, TILE - 6) + rot(west, TILE - 7) + rot(west, TILE - 8),
            cell_in[side],
            rot(east, TILE - 5) + rot(east, TILE - 6) + rot(east, TILE - 7)], axis=1)
        hs[side], _ = update(gates, cell)

    for k, tile in enumerate(interleaved(hs[0, :, TILE:2 * TILE], hs[1, :, TILE:2 * TILE])):
        g_top[k, 0:HID] = tile.astype(BF16)
    for k, tile in enumerate(interleaved(rest_in[0, CL:PA].astype(F32), rest_in[1, CL:PA].astype(F32))):
        g_top[k, HID:CT] = tile.astype(BF16)

    hidden, _ = update(windows(s_low, 0, 129, 9 * CL, wle), jnp.concatenate([lonf_in[0], lonf_in[1]], axis=1))
    for side in range(2):
        src = TILE - 1 if side == 0 else 0
        value = hidden[:, side * TILE:(side + 1) * TILE]
        lo = rot(hs[0, :, 2 * side * TILE:(2 * side + 1) * TILE], TILE - src)
        hi = rot(hs[1, :, 2 * side * TILE:(2 * side + 1) * TILE], 2 * TILE - 1 - src)
        sp[side, CT:CT + HID] = value.astype(BF16)
        shifted(sp, side, 0, HID, CT, value, lo, hi)
        value = lonb_in[side, 2 * CL:PK].astype(F32)
        lo = rot(cor_in[0, side, 0:HID].astype(F32), TILE - 4)
        hi = rot(cor_in[1, side, 0:HID].astype(F32), TILE - 5)
        sp[side, CT + HID:2 * CT] = value.astype(BF16)
        shifted(sp, side, HID, HID, CT, value, lo, hi)

    for copy in copies:
        copy.wait_send()
    for b in range(NB):
        for save in save_block(b):
            save.wait()
    saves[0].wait()


def lower_layer(fr, hl, ht, cl, wl, bl):
    anywhere = pl.BlockSpec(memory_space=pl.ANY)
    whole = pl.BlockSpec(memory_space=pltpu.VMEM)
    exchanged = [
        pltpu.VMEM((2, CL, TILE), BF16),
        pltpu.VMEM((2, PA, TILE), BF16),
        pltpu.VMEM((2, HID, TILE), F32),
        pltpu.VMEM((2, 2, CL, TILE), BF16),
        pltpu.VMEM((2, PK, TILE), BF16),
        pltpu.VMEM((2, HID, TILE), F32),
    ]
    return pl.pallas_call(
        lower_kernel,
        out_shape=(
            jax.ShapeDtypeStruct((TILE, HID, TILE), BF16),
            jax.ShapeDtypeStruct((TILE, HID, TILE), BF16),
            jax.ShapeDtypeStruct((NB, HID, BX, TILE), F32),
            jax.ShapeDtypeStruct((2, CT, TILE), BF16),
            jax.ShapeDtypeStruct((2, 3 * CT, TILE), BF16),
        ),
        in_specs=[anywhere] * 4 + [whole] * 2,
        out_specs=(anywhere, anywhere, anywhere, whole, whole),
        scratch_shapes=[
            pltpu.VMEM((CIN, TILE, TILE), BF16),
            pltpu.VMEM((HID, TILE, TILE), BF16),
            pltpu.VMEM((HID, TILE, TILE), BF16),
            pltpu.VMEM((NB, HID, PITCH, TILE), F32),
            pltpu.VMEM((TILE + 4, 3 * CL, TILE), BF16),
            pltpu.VMEM((2, TILE, HID, TILE), BF16),
            pltpu.VMEM((9 * CL, 3 * TILE), BF16),
            pltpu.VMEM((2, HID, 3 * TILE), F32),
            pltpu.VMEM((2, CL, TILE), BF16),
            pltpu.VMEM((4 * HID, 9 * CL + 48), BF16),
            pltpu.VMEM((HID * BX, TILE), F32),
            pltpu.VMEM((HID * 8, TILE), F32),
            *exchanged,
            *exchanged,
            pltpu.SemaphoreType.DMA((3 + NB,)),
            pltpu.SemaphoreType.DMA((3, NB)),
            pltpu.SemaphoreType.DMA((3, 2)),
            pltpu.SemaphoreType.DMA((3, 2)),
            pltpu.SemaphoreType.DMA((2, 2)),
            pltpu.SemaphoreType.DMA((2, 2)),
            pltpu.SemaphoreType.DMA((2, 2)),
            pltpu.SemaphoreType.DMA((2, 2)),
        ],
        compiler_params=pltpu.CompilerParams(
            collective_id=0, has_side_effects=True, vmem_limit_bytes=60 * 1024 * 1024
        ),
        name="lower_layer",
    )(fr, hl, ht, cl, wl, bl)


def upper_kernel(
    t_hid, t_ht, co_in, ct, g_top, sp, wt, bt,
    th, ho, co, cto,
    ctv, cov, hov, thv, s_top, wte, rows,
    sem_in, sem_out,
):
    def span(b):
        return pl.ds(pl.multiple_of(b * BX, BX), BX)

    def load(k, b):
        if k >= 2:
            source, dest = (ct.at[:, span(b), :], ctv.at[b, :, 0:BX, :]) if k == 2 else (co_in.at[b], cov.at[b])
            return pltpu.make_async_copy(source, dest, sem_in.at[k, b])
        source = (t_hid, t_ht)[k]
        at = CT + k * HID
        return pltpu.make_async_copy(
            source.at[span(b)], s_top.at[pl.ds(b * BX + 1, BX), at:at + HID, :], sem_in.at[k, b])

    def save(k, b):
        source, dest = ((hov, ho), (thv, th), (ctv, cto), (cov, co))[k]
        source = source.at[b, :, 0:BX, :] if k == 2 else source.at[b]
        return pltpu.make_async_copy(source, dest.at[:, span(b), :], sem_out.at[k, b])

    for b in range(2):
        for k in range(4):
            load(k, b).start()

    extended_weights(wte, wt[...].astype(F32), bt[...], 9 * CT)
    s_top[0] = sp[0]
    s_top[TILE + 1] = sp[1]

    def shift_row(x, parity):
        halo = rot(g_top[parity].astype(F32), lax.rem(TILE - x, TILE))
        shifted(s_top, x + 1, 0, CT, CT, s_top[x + 1, CT:2 * CT].astype(F32), halo, halo)

    for k in range(2):
        load(k, 0).wait()
    for b in range(2, 4):
        for k in range(4):
            load(k, b).start()

    def shift_first(i, carry):
        for j in range(4):
            shift_row(4 * i + j, j % 2)
        return carry

    lax.fori_loop(0, BX // 4, shift_first, 0)

    def top_rows(b, i, shift):
        x = b * BX + i
        cells = ctv.at[b].reshape(HID * PITCH, TILE)
        cell = jnp.concatenate([cells[pl.ds(i + j, HID, stride=PITCH), :] for j in range(2)], axis=1)
        hidden, cell = update(windows(s_top, x, x + 1, 9 * CT, wte), cell)
        for j in range(2):
            if shift:
                shift_row(x + BX + j, j)
            part = slice(j * TILE, (j + 1) * TILE)
            cells[pl.ds(i + j, HID, stride=PITCH), :] = cell[:, part]
            rows[i + j] = hidden[:, part].astype(BF16)

    def top_block(b, shift, before):
        hov[b] = jnp.swapaxes(s_top[pl.ds(b * BX + 1, BX), CT:CT + HID], 0, 1)
        thv[before] = jnp.swapaxes(rows[...], 0, 1)
        for i in range(0, BX, 2):
            top_rows(b, i, shift)
        for k in (0, 2, 3):
            save(k, b).start()

    def arrived(k, b):
        for kind in k:
            load(kind, b).wait()

    def top_step(step, carry):
        b = 2 * step

        @pl.when(step > 0)
        def _():
            save(1, b - 2).start()

        @pl.when(b + 4 < NB)
        def _():
            for k in range(4):
                load(k, b + 4).start()
                load(k, b + 5).start()

        arrived((2, 3), b)
        arrived((0, 1, 2, 3), b + 1)
        arrived((0, 1), b + 2)
        before = jnp.maximum(b - 1, 0)
        top_block(b, True, before)
        top_block(b + 1, True, b)

        @pl.when(step > 0)
        def _():
            save(1, b - 1).start()
        return carry

    rows[...] = jnp.zeros(rows.shape, BF16)
    lax.fori_loop(0, NB // 2 - 1, top_step, 0)
    b = NB - 2
    save(1, b - 2).start()
    arrived((2, 3), b)
    arrived((0, 1, 2, 3), b + 1)
    top_block(b, True, b - 1)
    save(1, b - 1).start()
    top_block(b + 1, False, b)
    save(1, b).start()
    thv[b + 1] = jnp.swapaxes(rows[...], 0, 1)
    save(1, b + 1).start()
    for k in range(4):
        for b in range(NB):
            save(k, b).wait()


def upper_layer(t_hid, t_ht, co, ct, g_top, sp, wt, bt):
    anywhere = pl.BlockSpec(memory_space=pl.ANY)
    whole = pl.BlockSpec(memory_space=pltpu.VMEM)
    field = (HID, TILE, TILE)
    return pl.pallas_call(
        upper_kernel,
        out_shape=(
            jax.ShapeDtypeStruct(field, BF16),
            jax.ShapeDtypeStruct(field, BF16),
            jax.ShapeDtypeStruct(field, F32),
            jax.ShapeDtypeStruct(field, F32),
        ),
        in_specs=[anywhere] * 4 + [whole] * 4,
        out_specs=(anywhere,) * 4,
        scratch_shapes=[
            pltpu.VMEM((NB, HID, PITCH, TILE), F32),
            pltpu.VMEM((NB, HID, BX, TILE), F32),
            pltpu.VMEM((NB, HID, BX, TILE), BF16),
            pltpu.VMEM((NB, HID, BX, TILE), BF16),
            pltpu.VMEM((TILE + 2, 3 * CT, TILE), BF16),
            pltpu.VMEM((4 * HID, 9 * CT + TILE), BF16),
            pltpu.VMEM((BX, HID, TILE), BF16),
            pltpu.SemaphoreType.DMA((4, NB)),
            pltpu.SemaphoreType.DMA((4, NB)),
        ],
        compiler_params=pltpu.CompilerParams(vmem_limit_bytes=60 * 1024 * 1024),
        name="upper_layer",
    )(t_hid, t_ht, co, ct, g_top, sp, wt, bt)


def body(frames, hidden_low, cell_low, hidden_top, cell_top, weight_low, bias_low, weight_top, bias_top):
    fr = frames.reshape(frames.shape[2:])
    hl, cl, ht, ct = (field.reshape(field.shape[1:]) for field in (hidden_low, cell_low, hidden_top, cell_top))
    t_hid, t_ht, co, g_top, sp = lower_layer(fr, hl, ht, cl, weight_low.T, bias_low.reshape(1, -1))
    th, ho, co, cto = upper_layer(t_hid, t_ht, co, ct, g_top, sp, weight_top, bias_top.reshape(1, -1))
    return th[None, None], ho[None], co[None], cto[None]


def solution(mesh):
    field = P(None, None, "lon", "lat")
    frame = P(None, None, None, "lon", "lat")
    return jax.shard_map(
        body,
        mesh=mesh,
        in_specs=(frame, field, field, field, field, P(), P(), P(), P()),
        out_specs=(frame, field, field, field),
        check_vma=False,
    )
```

```python
import functools

import jax
import jax.numpy as jnp
from jax import lax
from jax.experimental import pallas as pl
from jax.experimental.pallas import tpu as pltpu
from jax.sharding import PartitionSpec as P

CIN, HID, TILE, BX = 16, 64, 128, 16
CL = CIN + HID
CT = 2 * HID
NB = TILE // BX
AHEAD = 4
PITCH = 24
PK = 2 * CL + HID
PA = CL + HID
F32, BF16 = jnp.float32, jnp.bfloat16
MESH = pl.DeviceIdType.MESH


def rot(block, shift):
    return pltpu.roll(block, shift % block.shape[1] if isinstance(shift, int) else shift, 1)


def lanes(shape):
    return lax.broadcasted_iota(jnp.int32, shape, 1)


def update(gates, cell):
    take = jnp.tanh(gates[0:HID])
    keep = jnp.tanh(gates[HID:2 * HID])
    cand = jnp.tanh(gates[2 * HID:3 * HID])
    show = jnp.tanh(gates[3 * HID:4 * HID])
    cell = 0.5 * ((keep + 1.0) * cell + (take + 1.0) * cand)
    return 0.5 * (show + 1.0) * jnp.tanh(cell), cell


def extended_weights(out, weight, bias, width):
    gate = lax.broadcasted_iota(jnp.int32, (4 * HID, 1), 0)
    half = jnp.where((gate >= 2 * HID) & (gate < 3 * HID), 1.0, 0.5)
    out[:, 0:width] = (weight * half).astype(BF16)
    spread = jnp.transpose(jnp.broadcast_to(bias, (TILE, 4 * HID))) * half
    high = spread.astype(BF16).astype(F32)
    mid = (spread - high).astype(BF16).astype(F32)
    low = spread - high - mid
    lane = lanes((4 * HID, TILE))
    tail = jnp.where(lane == 0, high, jnp.where(lane == 1, mid, jnp.where(lane == 2, low, 0.0)))
    out[:, width:width + 16] = tail[:, 0:16].astype(BF16)


def shifted(dest, at, base, width, stride, value, lane_lo, lane_hi):
    lane = lanes(value.shape)
    down = jnp.where(lane == 0, lane_lo, rot(value, 1))
    up = jnp.where(lane == TILE - 1, lane_hi, rot(value, TILE - 1))
    dest[at, base:base + width] = down.astype(BF16)
    dest[at, 2 * stride + base:2 * stride + base + width] = up.astype(BF16)


def interleaved(low, high):
    even = lax.rem(lanes(low.shape), 2) == 0
    high = rot(high, TILE - 1)
    return jnp.where(even, low, high), jnp.where(even, high, low)


def windows(source, first, second, width, weights):
    pair = jnp.concatenate(
        [source[pl.ds(first, 3)].reshape(width, TILE), source[pl.ds(second, 3)].reshape(width, TILE)], axis=1
    )
    ones = jnp.ones((16, 2 * TILE), BF16)
    return jnp.dot(weights[:, 0:width + 16], jnp.concatenate([pair, ones], axis=0), preferred_element_type=F32)


def lower_kernel(
    fr, hl, ht, cl, wl, bl,
    t_hid, t_ht, co, g_top, sp,
    frv, hlv, htv, clv, s_low, hid, strip, hs, g_low, wle, tmp, ctmp,
    near_out, rest_out, cell_out, cor_out, lonb_out, lonf_out,
    near_in, rest_in, cell_in, cor_in, lonb_in, lonf_in,
    sem_in, sem_out, send_lat, recv_lat, send_cor, recv_cor, send_lon, recv_lon,
):
    nlon, nlat = lax.axis_size("lon"), lax.axis_size("lat")
    lon, lat = lax.axis_index("lon"), lax.axis_index("lat")
    loads = [
        pltpu.make_async_copy(src, dst, sem_in.at[k])
        for k, (src, dst) in enumerate(((fr, frv), (hl, hlv), (ht, htv)))
    ] + [
        pltpu.make_async_copy(cl.at[:, b * BX:(b + 1) * BX, :], clv.at[b, :, 0:BX, :], sem_in.at[3 + b]) for b in range(NB)
    ]
    for load in loads[0:2]:
        load.start()

    polars = [lat == 0, lat == nlat - 1]
    lat_targets, slots = [], []
    for side in range(2):
        to_lat = jnp.where(polars[side], lat, lat + (-1 if side == 0 else 1))
        shift = jnp.where(polars[side], nlon // 2, 0)
        slots.append(jnp.where(polars[side], side, 1 - side))
        lat_targets.append([(lax.rem(lon + shift + step + nlon, nlon), to_lat) for step in (-1, 0, 1)])
    lon_targets = [(lax.rem(lon + step + nlon, nlon), lat) for step in (-1, 1)]

    barrier = pltpu.get_barrier_semaphore()
    for target in lat_targets[0] + lat_targets[1] + lon_targets:
        pl.semaphore_signal(barrier, inc=1, device_id=target, device_id_type=MESH)

    row = lax.broadcasted_iota(jnp.int32, (16, TILE), 0)
    col = lax.broadcasted_iota(jnp.int32, (16, TILE), 1)
    wanted = jnp.where(row == 1, 1, jnp.where(row == 2, TILE - 1, jnp.where(row == 3, TILE - 2, 0)))
    pick = jnp.where((col == wanted) & (row < 4), 1.0, 0.0).astype(BF16)

    def columns(field, base, k):
        at = pl.multiple_of(k * 8, 8)
        found = lax.dot_general(
            pick, field[pl.ds(at, 8)].reshape(8 * TILE, TILE), (((1,), (1,)), ((), ())),
            preferred_element_type=F32,
        )
        for j in range(8):
            tmp[pl.ds(pl.multiple_of((base + at + j) * 8, 8), 8), :] = found[0:8, j * TILE:(j + 1) * TILE]

    def rows(field, count, base, whole):
        for side in range(2):
            start = 0 if side == 0 else TILE - BX
            tmp[0:count * BX, :] = field[:, start:start + BX, :].astype(F32).reshape(count * BX, TILE)
            first, second = (0, 1) if side == 0 else (BX - 1, BX - 2)
            lonb_out[side, base:base + count] = tmp[pl.ds(first, count, stride=BX), :].astype(BF16)
            if whole:
                lonb_out[side, CL + base:CL + base + count] = tmp[pl.ds(second, count, stride=BX), :].astype(BF16)

    copies = []

    def send(src, dst, send_sem, recv_sem, target):
        copies.append(pltpu.make_async_remote_copy(
            src_ref=src, dst_ref=dst, send_sem=send_sem, recv_sem=recv_sem,
            device_id=target, device_id_type=MESH))
        copies[-1].start()

    def received(src, dst, send_sem, recv_sem):
        pltpu.make_async_remote_copy(
            src_ref=src, dst_ref=dst, send_sem=send_sem, recv_sem=recv_sem,
            device_id=lon_targets[0], device_id_type=MESH).wait_recv()

    for load in loads[0:2]:
        load.wait()
    for load in loads[2:]:
        load.start()
    for k in range(CIN // 8):
        columns(frv, 0, k)

    def hidden_columns(k, carry):
        columns(hlv, CIN, 2 * k)
        columns(hlv, CIN, 2 * k + 1)
        return carry

    lax.fori_loop(0, HID // 16, hidden_columns, 0)
    for side in range(2):
        near_out[side] = tmp[pl.ds(2 * side, CL, stride=8), :].astype(BF16)
        rest_out[side, 0:CL] = tmp[pl.ds(2 * side + 1, CL, stride=8), :].astype(BF16)
    pl.semaphore_wait(barrier, 8)
    for side in range(2):
        send(near_out.at[side], near_in.at[slots[side]], send_lat.at[0, side], recv_lat.at[0, slots[side]],
             lat_targets[side][1])

    rows(frv, CIN, 0, True)
    rows(hlv, HID, CIN, True)
    extended_weights(wle, jnp.transpose(wl[...].astype(F32)), bl[...], 9 * CL)
    loads[2].wait()
    rows(htv, HID, 2 * CL, False)
    for side in range(2):
        send(lonb_out.at[side], lonb_in.at[1 - side], send_lon.at[0, side], recv_lon.at[0, 1 - side],
             lon_targets[side])
    for load in loads[3:]:
        load.wait()

    def relayout(b, carry):
        at = pl.multiple_of(b * BX, BX)
        columns(htv, 0, b)
        for j in range(8):
            turned = jnp.transpose(jnp.concatenate([clv[k, b * 8 + j, 0:BX] for k in range(NB)], axis=0))
            ctmp[pl.ds(pl.multiple_of((b * 8 + j) * 8, 8), 8), :] = jnp.where(
                lax.broadcasted_iota(jnp.int32, (8, TILE), 0) < 4, turned[0:8], turned[TILE - 8:TILE])
        s_low[pl.ds(at + 2, BX), CL:CL + CIN] = jnp.swapaxes(frv[:, pl.ds(at, BX), :], 0, 1)
        s_low[pl.ds(at + 2, BX), CL + CIN:2 * CL] = jnp.swapaxes(hlv[:, pl.ds(at, BX), :], 0, 1)
        hid[1, pl.ds(at, BX)] = jnp.swapaxes(htv[:, pl.ds(at, BX), :], 0, 1)
        return carry

    lax.fori_loop(0, NB, relayout, 0)
    for side in range(2):
        rest_out[side, CL:PA] = tmp[pl.ds(2 * side, HID, stride=8), :].astype(BF16)
        send(rest_out.at[side], rest_in.at[slots[side]], send_lat.at[1, side], recv_lat.at[1, slots[side]],
             lat_targets[side][1])
        cell_out[side] = ctmp[pl.ds(7 * side, HID, stride=8), :]
    for side in range(2):
        block, first = (0, 0) if side == 0 else (NB - 1, BX - 1)
        lonf_out[side] = clv.at[block].reshape(HID * PITCH, TILE)[pl.ds(first, HID, stride=PITCH), :]

    for side in range(2):
        send(cell_out.at[side], cell_in.at[slots[side]], send_lat.at[2, side], recv_lat.at[2, slots[side]],
             lat_targets[side][1])
        send(lonf_out.at[side], lonf_in.at[1 - side], send_lon.at[1, side], recv_lon.at[1, 1 - side],
             lon_targets[side])

    saves = [pltpu.make_async_copy(hid.at[1], t_ht, sem_out.at[0, 0])]
    saves[0].start()

    for slot in range(2):
        received(near_out.at[0], near_in.at[slot], send_lat.at[0, slot], recv_lat.at[0, slot])
    for k, tile in enumerate(interleaved(near_in[0].astype(F32), near_in[1].astype(F32))):
        g_low[k] = tile.astype(BF16)

    def shift_row(x, parity):
        halo = rot(g_low[parity].astype(F32), lax.rem(TILE - x, TILE))
        shifted(s_low, x + 2, 0, CL, CL, s_low[x + 2, CL:2 * CL].astype(F32), halo, halo)

    for row in range(BX - 1, BX + AHEAD):
        shift_row(row, row % 2)

    def low_rows(b, i):
        x = b * BX + i
        ahead = (x + AHEAD) % TILE if isinstance(b, int) else x + AHEAD
        cells = clv.at[b].reshape(HID * PITCH, TILE)
        cell = jnp.concatenate([cells[pl.ds(i + j, HID, stride=PITCH), :] for j in range(2)], axis=1)
        hidden, cell = update(windows(s_low, x + 1, x + 2, 9 * CL, wle), cell)
        for j in range(2):
            shift_row(ahead + j, j)
            part = slice(j * TILE, (j + 1) * TILE)
            cells[pl.ds(i + j, HID, stride=PITCH), :] = cell[:, part]
            hid[0, x + j] = hidden[:, part].astype(BF16)

    def save_block(b):
        at = pl.multiple_of(b * BX, BX)
        return (
            pltpu.make_async_copy(clv.at[b, :, 0:BX, :], co.at[b], sem_out.at[1, b]),
            pltpu.make_async_copy(hid.at[0, pl.ds(at, BX)], t_hid.at[pl.ds(at, BX)], sem_out.at[2, b]),
        )

    def low_block(b):
        for i in range(0, BX, 2):
            low_rows(b, i)
        for save in save_block(b):
            save.start()

    def low_step(k, carry):
        low_block(2 * k + 1)
        low_block(2 * k + 2)
        return carry

    low_block(1)
    for side in range(2):
        near = near_out[side].astype(F32)
        rest = rest_out[side].astype(F32)
        cell = cell_out[side]
        high = cell.astype(BF16).astype(F32)
        mid = (cell - high).astype(BF16).astype(F32)
        low = cell - high - mid
        pad = jnp.zeros((CL - HID, TILE), F32)
        wide = [near, near, rest[0:CL], rest[0:CL]] + [
            jnp.concatenate([part, pad], axis=0) for part in (rest[CL:PA], high, mid, low)]
        for step in range(2):
            ends = (0, 1) if step == 0 else (TILE - 1, TILE - 2)
            source = (ends[0], ends[1], ends[0], ends[1], ends[0], ends[0], ends[0], ends[0])
            lane = lanes((CL, TILE))
            package = jnp.zeros((CL, TILE), F32)
            for k in range(8):
                package = jnp.where(lane == k, rot(wide[k], k - source[k] + TILE), package)
            cor_out[side, step] = package.astype(BF16)
    for side in range(2):
        for step in range(2):
            send(cor_out.at[side, step], cor_in.at[slots[side], 1 - step], send_cor.at[side, step],
                 recv_cor.at[slots[side], 1 - step], lat_targets[side][2 * step])
    low_block(2)
    lax.fori_loop(1, NB // 2 - 1, low_step, 0)

    for slot in range(2):
        received(lonb_out.at[0], lonb_in.at[slot], send_lon.at[0, slot], recv_lon.at[0, slot])
        for step in range(2):
            received(cor_out.at[0, 0], cor_in.at[slot, step], send_cor.at[slot, step], recv_cor.at[slot, step])

    for at, side, far in ((1, 0, 0), (0, 0, 1), (130, 1, 0), (131, 1, 1)):
        value = lonb_in[side, far * CL:far * CL + CL].astype(F32)
        lo = rot(cor_in[0, side].astype(F32), TILE - far)
        hi = rot(cor_in[1, side].astype(F32), TILE - 1 - far)
        s_low[at, CL:2 * CL] = value.astype(BF16)
        shifted(s_low, at, 0, CL, CL, value, lo, hi)
    low_block(NB - 1)
    low_block(0)

    for slot in range(2):
        received(rest_out.at[0], rest_in.at[slot], send_lat.at[1, slot], recv_lat.at[1, slot])
        received(cell_out.at[0], cell_in.at[slot], send_lat.at[2, slot], recv_lat.at[2, slot])
        received(lonf_out.at[0], lonf_in.at[slot], send_lon.at[1, slot], recv_lon.at[1, slot])
    for side in range(2):
        lane = lanes((CL, TILE))
        west = cor_in[side, 0].astype(F32)
        east = cor_in[side, 1].astype(F32)
        near = jnp.concatenate([
            jnp.where(lane == TILE - 1, rot(west, TILE - 1), rot(west, TILE - 3)),
            near_in[side].astype(F32), east], axis=1)
        far = jnp.concatenate([
            jnp.where(lane == TILE - 1, rot(west, TILE - 3), rot(west, TILE - 5)),
            rest_in[side, 0:CL].astype(F32), rot(east, TILE - 2)], axis=1)
        edge = 0 if side == 0 else TILE - 1
        parts = [lonb_in[0, 0:CL], lonb_in[0, CL:2 * CL], lonb_in[1, 0:CL], lonb_in[1, CL:2 * CL]]
        parts = [part.astype(F32) for part in parts]
        mine = jnp.concatenate([
            jnp.where(lane == TILE - 1, rot(parts[0], TILE - 1 - edge), rot(parts[1], 2 * TILE - 2 - edge)),
            near_out[side].astype(F32),
            jnp.where(lane == 0, rot(parts[2], TILE - edge), rot(parts[3], TILE + 1 - edge))], axis=1)
        outer = jnp.where(polars[side], mine, far)
        inner = jnp.where(polars[side], far, mine)
        order = (outer, near, inner) if side == 0 else (inner, near, outer)
        for e in range(3):
            for a in range(3):
                at = (3 * a + e) * CL
                strip[at:at + CL, :] = rot(order[e], 1 - a).astype(BF16)
        gates = jnp.dot(
            wle[:, 0:9 * CL + 16],
            jnp.concatenate([strip[...], jnp.ones((16, 3 * TILE), BF16)], axis=0),
            preferred_element_type=F32,
        )
        west, east = west[0:HID], east[0:HID]
        cell = jnp.concatenate([
            rot(west, TILE - 6) + rot(west, TILE - 7) + rot(west, TILE - 8),
            cell_in[side],
            rot(east, TILE - 5) + rot(east, TILE - 6) + rot(east, TILE - 7)], axis=1)
        hs[side], _ = update(gates, cell)

    for k, tile in enumerate(interleaved(hs[0, :, TILE:2 * TILE], hs[1, :, TILE:2 * TILE])):
        g_top[k, 0:HID] = tile.astype(BF16)
    for k, tile in enumerate(interleaved(rest_in[0, CL:PA].astype(F32), rest_in[1, CL:PA].astype(F32))):
        g_top[k, HID:CT] = tile.astype(BF16)

    hidden, _ = update(windows(s_low, 0, 129, 9 * CL, wle), jnp.concatenate([lonf_in[0], lonf_in[1]], axis=1))
    for side in range(2):
        src = TILE - 1 if side == 0 else 0
        value = hidden[:, side * TILE:(side + 1) * TILE]
        lo = rot(hs[0, :, 2 * side * TILE:(2 * side + 1) * TILE], TILE - src)
        hi = rot(hs[1, :, 2 * side * TILE:(2 * side + 1) * TILE], 2 * TILE - 1 - src)
        sp[side, CT:CT + HID] = value.astype(BF16)
        shifted(sp, side, 0, HID, CT, value, lo, hi)
        value = lonb_in[side, 2 * CL:PK].astype(F32)
        lo = rot(cor_in[0, side, 0:HID].astype(F32), TILE - 4)
        hi = rot(cor_in[1, side, 0:HID].astype(F32), TILE - 5)
        sp[side, CT + HID:2 * CT] = value.astype(BF16)
        shifted(sp, side, HID, HID, CT, value, lo, hi)

    for copy in copies:
        copy.wait_send()
    for b in range(NB):
        for save in save_block(b):
            save.wait()
    saves[0].wait()


def lower_layer(fr, hl, ht, cl, wl, bl):
    anywhere = pl.BlockSpec(memory_space=pl.ANY)
    whole = pl.BlockSpec(memory_space=pltpu.VMEM)
    exchanged = [
        pltpu.VMEM((2, CL, TILE), BF16),
        pltpu.VMEM((2, PA, TILE), BF16),
        pltpu.VMEM((2, HID, TILE), F32),
        pltpu.VMEM((2, 2, CL, TILE), BF16),
        pltpu.VMEM((2, PK, TILE), BF16),
        pltpu.VMEM((2, HID, TILE), F32),
    ]
    return pl.pallas_call(
        lower_kernel,
        out_shape=(
            jax.ShapeDtypeStruct((TILE, HID, TILE), BF16),
            jax.ShapeDtypeStruct((TILE, HID, TILE), BF16),
            jax.ShapeDtypeStruct((NB, HID, BX, TILE), F32),
            jax.ShapeDtypeStruct((2, CT, TILE), BF16),
            jax.ShapeDtypeStruct((2, 3 * CT, TILE), BF16),
        ),
        in_specs=[anywhere] * 4 + [whole] * 2,
        out_specs=(anywhere, anywhere, anywhere, whole, whole),
        scratch_shapes=[
            pltpu.VMEM((CIN, TILE, TILE), BF16),
            pltpu.VMEM((HID, TILE, TILE), BF16),
            pltpu.VMEM((HID, TILE, TILE), BF16),
            pltpu.VMEM((NB, HID, PITCH, TILE), F32),
            pltpu.VMEM((TILE + 4, 3 * CL, TILE), BF16),
            pltpu.VMEM((2, TILE, HID, TILE), BF16),
            pltpu.VMEM((9 * CL, 3 * TILE), BF16),
            pltpu.VMEM((2, HID, 3 * TILE), F32),
            pltpu.VMEM((2, CL, TILE), BF16),
            pltpu.VMEM((4 * HID, 9 * CL + 48), BF16),
            pltpu.VMEM((HID * BX, TILE), F32),
            pltpu.VMEM((HID * 8, TILE), F32),
            *exchanged,
            *exchanged,
            pltpu.SemaphoreType.DMA((3 + NB,)),
            pltpu.SemaphoreType.DMA((3, NB)),
            pltpu.SemaphoreType.DMA((3, 2)),
            pltpu.SemaphoreType.DMA((3, 2)),
            pltpu.SemaphoreType.DMA((2, 2)),
            pltpu.SemaphoreType.DMA((2, 2)),
            pltpu.SemaphoreType.DMA((2, 2)),
            pltpu.SemaphoreType.DMA((2, 2)),
        ],
        compiler_params=pltpu.CompilerParams(
            collective_id=0, has_side_effects=True, vmem_limit_bytes=60 * 1024 * 1024
        ),
        name="lower_layer",
    )(fr, hl, ht, cl, wl, bl)


def upper_kernel(
    t_hid, t_ht, co_in, ct, g_top, sp, wt, bt,
    th, ho, co, cto,
    ctv, cov, hov, thv, s_top, wte, rows,
    sem_in, sem_out,
):
    def span(b):
        return pl.ds(pl.multiple_of(b * BX, BX), BX)

    def load(k, b):
        if k >= 2:
            source, dest = (ct.at[:, span(b), :], ctv.at[b, :, 0:BX, :]) if k == 2 else (co_in.at[b], cov.at[b])
            return pltpu.make_async_copy(source, dest, sem_in.at[k, b])
        source = (t_hid, t_ht)[k]
        at = CT + k * HID
        return pltpu.make_async_copy(
            source.at[span(b)], s_top.at[pl.ds(b * BX + 1, BX), at:at + HID, :], sem_in.at[k, b])

    def save(k, b):
        source, dest = ((hov, ho), (thv, th), (ctv, cto), (cov, co))[k]
        source = source.at[b, :, 0:BX, :] if k == 2 else source.at[b]
        return pltpu.make_async_copy(source, dest.at[:, span(b), :], sem_out.at[k, b])

    for b in range(2):
        for k in range(4):
            load(k, b).start()

    extended_weights(wte, wt[...].astype(F32), bt[...], 9 * CT)
    s_top[0] = sp[0]
    s_top[TILE + 1] = sp[1]

    def shift_row(x, parity):
        halo = rot(g_top[parity].astype(F32), lax.rem(TILE - x, TILE))
        shifted(s_top, x + 1, 0, CT, CT, s_top[x + 1, CT:2 * CT].astype(F32), halo, halo)

    for k in range(2):
        load(k, 0).wait()
    for b in range(2, 4):
        for k in range(4):
            load(k, b).start()

    for row in range(AHEAD):
        shift_row(row, row % 2)

    def top_rows(b, i, shift):
        x = b * BX + i
        cells = ctv.at[b].reshape(HID * PITCH, TILE)
        cell = jnp.concatenate([cells[pl.ds(i + j, HID, stride=PITCH), :] for j in range(2)], axis=1)
        hidden, cell = update(windows(s_top, x, x + 1, 9 * CT, wte), cell)
        for j in range(2):
            if shift or i + AHEAD < BX:
                shift_row(x + AHEAD + j, j)
            part = slice(j * TILE, (j + 1) * TILE)
            cells[pl.ds(i + j, HID, stride=PITCH), :] = cell[:, part]
            rows[i + j] = hidden[:, part].astype(BF16)

    def top_block(b, shift, before):
        hov[b] = jnp.swapaxes(s_top[pl.ds(b * BX + 1, BX), CT:CT + HID], 0, 1)
        thv[before] = jnp.swapaxes(rows[...], 0, 1)
        for i in range(0, BX, 2):
            top_rows(b, i, shift)
        for k in (0, 2, 3):
            save(k, b).start()

    def arrived(k, b):
        for kind in k:
            load(kind, b).wait()

    def top_step(step, carry):
        b = 2 * step

        @pl.when(step > 0)
        def _():
            save(1, b - 2).start()

        @pl.when(b + 4 < NB)
        def _():
            for k in range(4):
                load(k, b + 4).start()
                load(k, b + 5).start()

        arrived((2, 3), b)
        arrived((0, 1), b + 1)
        before = jnp.maximum(b - 1, 0)
        top_block(b, True, before)
        arrived((2, 3), b + 1)
        arrived((0, 1), b + 2)
        top_block(b + 1, True, b)

        @pl.when(step > 0)
        def _():
            save(1, b - 1).start()
        return carry

    rows[...] = jnp.zeros(rows.shape, BF16)
    lax.fori_loop(0, NB // 2 - 1, top_step, 0)
    b = NB - 2
    save(1, b - 2).start()
    arrived((2, 3), b)
    arrived((0, 1, 2, 3), b + 1)
    top_block(b, True, b - 1)
    save(1, b - 1).start()
    top_block(b + 1, False, b)
    save(1, b).start()
    thv[b + 1] = jnp.swapaxes(rows[...], 0, 1)
    save(1, b + 1).start()
    for k in range(4):
        for b in range(NB):
            save(k, b).wait()


def upper_layer(t_hid, t_ht, co, ct, g_top, sp, wt, bt):
    anywhere = pl.BlockSpec(memory_space=pl.ANY)
    whole = pl.BlockSpec(memory_space=pltpu.VMEM)
    field = (HID, TILE, TILE)
    return pl.pallas_call(
        upper_kernel,
        out_shape=(
            jax.ShapeDtypeStruct(field, BF16),
            jax.ShapeDtypeStruct(field, BF16),
            jax.ShapeDtypeStruct(field, F32),
            jax.ShapeDtypeStruct(field, F32),
        ),
        in_specs=[anywhere] * 4 + [whole] * 4,
        out_specs=(anywhere,) * 4,
        scratch_shapes=[
            pltpu.VMEM((NB, HID, PITCH, TILE), F32),
            pltpu.VMEM((NB, HID, BX, TILE), F32),
            pltpu.VMEM((NB, HID, BX, TILE), BF16),
            pltpu.VMEM((NB, HID, BX, TILE), BF16),
            pltpu.VMEM((TILE + 2, 3 * CT, TILE), BF16),
            pltpu.VMEM((4 * HID, 9 * CT + TILE), BF16),
            pltpu.VMEM((BX, HID, TILE), BF16),
            pltpu.SemaphoreType.DMA((4, NB)),
            pltpu.SemaphoreType.DMA((4, NB)),
        ],
        compiler_params=pltpu.CompilerParams(vmem_limit_bytes=60 * 1024 * 1024),
        name="upper_layer",
    )(t_hid, t_ht, co, ct, g_top, sp, wt, bt)


def body(frames, hidden_low, cell_low, hidden_top, cell_top, weight_low, bias_low, weight_top, bias_top):
    fr = frames.reshape(frames.shape[2:])
    hl, cl, ht, ct = (field.reshape(field.shape[1:]) for field in (hidden_low, cell_low, hidden_top, cell_top))
    t_hid, t_ht, co, g_top, sp = lower_layer(fr, hl, ht, cl, weight_low.T, bias_low.reshape(1, -1))
    th, ho, co, cto = upper_layer(t_hid, t_ht, co, ct, g_top, sp, weight_top, bias_top.reshape(1, -1))
    return th[None, None], ho[None], co[None], cto[None]


def solution(mesh):
    field = P(None, None, "lon", "lat")
    frame = P(None, None, None, "lon", "lat")
    return jax.shard_map(
        body,
        mesh=mesh,
        in_specs=(frame, field, field, field, field, P(), P(), P(), P()),
        out_specs=(frame, field, field, field),
        check_vma=False,
    )
```

```python
import functools

import jax
import jax.numpy as jnp
from jax import lax
from jax.experimental import pallas as pl
from jax.experimental.pallas import tpu as pltpu
from jax.sharding import PartitionSpec as P

CIN, HID, TILE, BX = 16, 64, 128, 16
CL = CIN + HID
CT = 2 * HID
NB = TILE // BX
AHEAD = 4
PITCH = 24
PK = 2 * CL + HID
PA = CL + HID
F32, BF16 = jnp.float32, jnp.bfloat16
MESH = pl.DeviceIdType.MESH


def rot(block, shift):
    return pltpu.roll(block, shift % block.shape[1] if isinstance(shift, int) else shift, 1)


def lanes(shape):
    return lax.broadcasted_iota(jnp.int32, shape, 1)


def update(gates, cell):
    take = jnp.tanh(gates[0:HID])
    keep = jnp.tanh(gates[HID:2 * HID])
    cand = jnp.tanh(gates[2 * HID:3 * HID])
    show = jnp.tanh(gates[3 * HID:4 * HID])
    cell = 0.5 * ((keep + 1.0) * cell + (take + 1.0) * cand)
    return 0.5 * (show + 1.0) * jnp.tanh(cell), cell


def extended_weights(out, weight, bias, width):
    gate = lax.broadcasted_iota(jnp.int32, (4 * HID, 1), 0)
    half = jnp.where((gate >= 2 * HID) & (gate < 3 * HID), 1.0, 0.5)
    out[:, 0:width] = (weight * half).astype(BF16)
    spread = jnp.transpose(jnp.broadcast_to(bias, (TILE, 4 * HID))) * half
    high = spread.astype(BF16).astype(F32)
    mid = (spread - high).astype(BF16).astype(F32)
    low = spread - high - mid
    lane = lanes((4 * HID, TILE))
    tail = jnp.where(lane == 0, high, jnp.where(lane == 1, mid, jnp.where(lane == 2, low, 0.0)))
    out[:, width:width + 16] = tail[:, 0:16].astype(BF16)


def shifted(dest, at, base, width, stride, value, lane_lo, lane_hi):
    lane = lanes(value.shape)
    down = jnp.where(lane == 0, lane_lo, rot(value, 1))
    up = jnp.where(lane == TILE - 1, lane_hi, rot(value, TILE - 1))
    dest[at, base:base + width] = down.astype(BF16)
    dest[at, 2 * stride + base:2 * stride + base + width] = up.astype(BF16)


def interleaved(low, high):
    even = lax.rem(lanes(low.shape), 2) == 0
    high = rot(high, TILE - 1)
    return jnp.where(even, low, high), jnp.where(even, high, low)


def windows(source, first, second, width, weights):
    pair = jnp.concatenate(
        [source[pl.ds(first, 3)].reshape(width, TILE), source[pl.ds(second, 3)].reshape(width, TILE)], axis=1
    )
    ones = jnp.ones((16, 2 * TILE), BF16)
    return jnp.dot(weights[:, 0:width + 16], jnp.concatenate([pair, ones], axis=0), preferred_element_type=F32)


def lower_kernel(
    fr, hl, ht, cl, wl, bl,
    t_hid, t_ht, co, g_top, sp,
    frv, hlv, htv, clv, s_low, hid, strip, hs, g_low, wle, tmp, ctmp,
    near_out, rest_out, cell_out, cor_out, lonb_out, lonf_out,
    near_in, rest_in, cell_in, cor_in, lonb_in, lonf_in,
    sem_in, sem_out, send_lat, recv_lat, send_cor, recv_cor, send_lon, recv_lon,
):
    nlon, nlat = lax.axis_size("lon"), lax.axis_size("lat")
    lon, lat = lax.axis_index("lon"), lax.axis_index("lat")
    loads = [
        pltpu.make_async_copy(src, dst, sem_in.at[k])
        for k, (src, dst) in enumerate(((fr, frv), (hl, hlv), (ht, htv)))
    ] + [
        pltpu.make_async_copy(cl.at[:, b * BX:(b + 1) * BX, :], clv.at[b, :, 0:BX, :], sem_in.at[3 + b]) for b in range(NB)
    ]
    pieces = [
        pltpu.make_async_copy(hl.at[q:q + CIN], hlv.at[q:q + CIN], sem_in.at[3 + NB + q // CIN])
        for q in range(0, HID, CIN)
    ]
    for load in [loads[0]] + pieces:
        load.start()

    polars = [lat == 0, lat == nlat - 1]
    lat_targets, slots = [], []
    for side in range(2):
        to_lat = jnp.where(polars[side], lat, lat + (-1 if side == 0 else 1))
        shift = jnp.where(polars[side], nlon // 2, 0)
        slots.append(jnp.where(polars[side], side, 1 - side))
        lat_targets.append([(lax.rem(lon + shift + step + nlon, nlon), to_lat) for step in (-1, 0, 1)])
    lon_targets = [(lax.rem(lon + step + nlon, nlon), lat) for step in (-1, 1)]

    barrier = pltpu.get_barrier_semaphore()
    for target in lat_targets[0] + lat_targets[1] + lon_targets:
        pl.semaphore_signal(barrier, inc=1, device_id=target, device_id_type=MESH)

    row = lax.broadcasted_iota(jnp.int32, (16, TILE), 0)
    col = lax.broadcasted_iota(jnp.int32, (16, TILE), 1)
    wanted = jnp.where(row == 1, 1, jnp.where(row == 2, TILE - 1, jnp.where(row == 3, TILE - 2, 0)))
    pick = jnp.where((col == wanted) & (row < 4), 1.0, 0.0).astype(BF16)

    def columns(field, base, k):
        at = pl.multiple_of(k * 8, 8)
        found = lax.dot_general(
            pick, field[pl.ds(at, 8)].reshape(8 * TILE, TILE), (((1,), (1,)), ((), ())),
            preferred_element_type=F32,
        )
        for j in range(8):
            tmp[pl.ds(pl.multiple_of((base + at + j) * 8, 8), 8), :] = found[0:8, j * TILE:(j + 1) * TILE]

    def rows(field, count, base, whole):
        for side in range(2):
            start = 0 if side == 0 else TILE - BX
            tmp[0:count * BX, :] = field[:, start:start + BX, :].astype(F32).reshape(count * BX, TILE)
            first, second = (0, 1) if side == 0 else (BX - 1, BX - 2)
            lonb_out[side, base:base + count] = tmp[pl.ds(first, count, stride=BX), :].astype(BF16)
            if whole:
                lonb_out[side, CL + base:CL + base + count] = tmp[pl.ds(second, count, stride=BX), :].astype(BF16)

    copies = []

    def send(src, dst, send_sem, recv_sem, target):
        copies.append(pltpu.make_async_remote_copy(
            src_ref=src, dst_ref=dst, send_sem=send_sem, recv_sem=recv_sem,
            device_id=target, device_id_type=MESH))
        copies[-1].start()

    def received(src, dst, send_sem, recv_sem):
        pltpu.make_async_remote_copy(
            src_ref=src, dst_ref=dst, send_sem=send_sem, recv_sem=recv_sem,
            device_id=lon_targets[0], device_id_type=MESH).wait_recv()

    loads[0].wait()
    for k in range(CIN // 8):
        columns(frv, 0, k)

    for q in range(HID // CIN):
        pieces[q].wait()
        if q == HID // CIN - 1:
            for load in loads[2:]:
                load.start()
        for k in range(CIN // 8):
            columns(hlv, CIN, q * (CIN // 8) + k)
    for side in range(2):
        near_out[side] = tmp[pl.ds(2 * side, CL, stride=8), :].astype(BF16)
        rest_out[side, 0:CL] = tmp[pl.ds(2 * side + 1, CL, stride=8), :].astype(BF16)
    pl.semaphore_wait(barrier, 8)
    for side in range(2):
        send(near_out.at[side], near_in.at[slots[side]], send_lat.at[0, side], recv_lat.at[0, slots[side]],
             lat_targets[side][1])

    rows(frv, CIN, 0, True)
    rows(hlv, HID, CIN, True)
    extended_weights(wle, jnp.transpose(wl[...].astype(F32)), bl[...], 9 * CL)
    loads[2].wait()
    rows(htv, HID, 2 * CL, False)
    for side in range(2):
        send(lonb_out.at[side], lonb_in.at[1 - side], send_lon.at[0, side], recv_lon.at[0, 1 - side],
             lon_targets[side])
    for load in loads[3:]:
        load.wait()

    def relayout(b, carry):
        at = pl.multiple_of(b * BX, BX)
        columns(htv, 0, b)
        for j in range(8):
            turned = jnp.transpose(jnp.concatenate([clv[k, b * 8 + j, 0:BX] for k in range(NB)], axis=0))
            ctmp[pl.ds(pl.multiple_of((b * 8 + j) * 8, 8), 8), :] = jnp.where(
                lax.broadcasted_iota(jnp.int32, (8, TILE), 0) < 4, turned[0:8], turned[TILE - 8:TILE])
        s_low[pl.ds(at + 2, BX), CL:CL + CIN] = jnp.swapaxes(frv[:, pl.ds(at, BX), :], 0, 1)
        s_low[pl.ds(at + 2, BX), CL + CIN:2 * CL] = jnp.swapaxes(hlv[:, pl.ds(at, BX), :], 0, 1)
        hid[1, pl.ds(at, BX)] = jnp.swapaxes(htv[:, pl.ds(at, BX), :], 0, 1)
        return carry

    lax.fori_loop(0, NB, relayout, 0)
    for side in range(2):
        rest_out[side, CL:PA] = tmp[pl.ds(2 * side, HID, stride=8), :].astype(BF16)
        send(rest_out.at[side], rest_in.at[slots[side]], send_lat.at[1, side], recv_lat.at[1, slots[side]],
             lat_targets[side][1])
        cell_out[side] = ctmp[pl.ds(7 * side, HID, stride=8), :]
    for side in range(2):
        block, first = (0, 0) if side == 0 else (NB - 1, BX - 1)
        lonf_out[side] = clv.at[block].reshape(HID * PITCH, TILE)[pl.ds(first, HID, stride=PITCH), :]

    for side in range(2):
        send(cell_out.at[side], cell_in.at[slots[side]], send_lat.at[2, side], recv_lat.at[2, slots[side]],
             lat_targets[side][1])
        send(lonf_out.at[side], lonf_in.at[1 - side], send_lon.at[1, side], recv_lon.at[1, 1 - side],
             lon_targets[side])

    saves = [pltpu.make_async_copy(hid.at[1], t_ht, sem_out.at[0, 0])]
    saves[0].start()

    for slot in range(2):
        received(near_out.at[0], near_in.at[slot], send_lat.at[0, slot], recv_lat.at[0, slot])
    for k, tile in enumerate(interleaved(near_in[0].astype(F32), near_in[1].astype(F32))):
        g_low[k] = tile.astype(BF16)

    def shift_row(x, parity):
        halo = rot(g_low[parity].astype(F32), lax.rem(TILE - x, TILE))
        shifted(s_low, x + 2, 0, CL, CL, s_low[x + 2, CL:2 * CL].astype(F32), halo, halo)

    for row in range(BX - 1, BX + AHEAD):
        shift_row(row, row % 2)

    def low_rows(b, i):
        x = b * BX + i
        ahead = (x + AHEAD) % TILE if isinstance(b, int) else x + AHEAD
        cells = clv.at[b].reshape(HID * PITCH, TILE)
        cell = jnp.concatenate([cells[pl.ds(i + j, HID, stride=PITCH), :] for j in range(2)], axis=1)
        hidden, cell = update(windows(s_low, x + 1, x + 2, 9 * CL, wle), cell)
        for j in range(2):
            shift_row(ahead + j, j)
            part = slice(j * TILE, (j + 1) * TILE)
            cells[pl.ds(i + j, HID, stride=PITCH), :] = cell[:, part]
            hid[0, x + j] = hidden[:, part].astype(BF16)

    def save_block(b):
        at = pl.multiple_of(b * BX, BX)
        return (
            pltpu.make_async_copy(clv.at[b, :, 0:BX, :], co.at[b], sem_out.at[1, b]),
            pltpu.make_async_copy(hid.at[0, pl.ds(at, BX)], t_hid.at[pl.ds(at, BX)], sem_out.at[2, b]),
        )

    def low_block(b):
        for i in range(0, BX, 2):
            low_rows(b, i)
        for save in save_block(b):
            save.start()

    def low_step(k, carry):
        low_block(2 * k + 1)
        low_block(2 * k + 2)
        return carry

    low_block(1)
    for side in range(2):
        near = near_out[side].astype(F32)
        rest = rest_out[side].astype(F32)
        cell = cell_out[side]
        high = cell.astype(BF16).astype(F32)
        mid = (cell - high).astype(BF16).astype(F32)
        low = cell - high - mid
        pad = jnp.zeros((CL - HID, TILE), F32)
        wide = [near, near, rest[0:CL], rest[0:CL]] + [
            jnp.concatenate([part, pad], axis=0) for part in (rest[CL:PA], high, mid, low)]
        for step in range(2):
            ends = (0, 1) if step == 0 else (TILE - 1, TILE - 2)
            source = (ends[0], ends[1], ends[0], ends[1], ends[0], ends[0], ends[0], ends[0])
            lane = lanes((CL, TILE))
            package = jnp.zeros((CL, TILE), F32)
            for k in range(8):
                package = jnp.where(lane == k, rot(wide[k], k - source[k] + TILE), package)
            cor_out[side, step] = package.astype(BF16)
    for side in range(2):
        for step in range(2):
            send(cor_out.at[side, step], cor_in.at[slots[side], 1 - step], send_cor.at[side, step],
                 recv_cor.at[slots[side], 1 - step], lat_targets[side][2 * step])
    low_block(2)
    lax.fori_loop(1, NB // 2 - 1, low_step, 0)

    for slot in range(2):
        received(lonb_out.at[0], lonb_in.at[slot], send_lon.at[0, slot], recv_lon.at[0, slot])
        for step in range(2):
            received(cor_out.at[0, 0], cor_in.at[slot, step], send_cor.at[slot, step], recv_cor.at[slot, step])

    for at, side, far in ((1, 0, 0), (0, 0, 1), (130, 1, 0), (131, 1, 1)):
        value = lonb_in[side, far * CL:far * CL + CL].astype(F32)
        lo = rot(cor_in[0, side].astype(F32), TILE - far)
        hi = rot(cor_in[1, side].astype(F32), TILE - 1 - far)
        s_low[at, CL:2 * CL] = value.astype(BF16)
        shifted(s_low, at, 0, CL, CL, value, lo, hi)
    low_block(NB - 1)
    low_block(0)

    for slot in range(2):
        received(rest_out.at[0], rest_in.at[slot], send_lat.at[1, slot], recv_lat.at[1, slot])
        received(cell_out.at[0], cell_in.at[slot], send_lat.at[2, slot], recv_lat.at[2, slot])
        received(lonf_out.at[0], lonf_in.at[slot], send_lon.at[1, slot], recv_lon.at[1, slot])
    for side in range(2):
        lane = lanes((CL, TILE))
        west = cor_in[side, 0].astype(F32)
        east = cor_in[side, 1].astype(F32)
        near = jnp.concatenate([
            jnp.where(lane == TILE - 1, rot(west, TILE - 1), rot(west, TILE - 3)),
            near_in[side].astype(F32), east], axis=1)
        far = jnp.concatenate([
            jnp.where(lane == TILE - 1, rot(west, TILE - 3), rot(west, TILE - 5)),
            rest_in[side, 0:CL].astype(F32), rot(east, TILE - 2)], axis=1)
        edge = 0 if side == 0 else TILE - 1
        parts = [lonb_in[0, 0:CL], lonb_in[0, CL:2 * CL], lonb_in[1, 0:CL], lonb_in[1, CL:2 * CL]]
        parts = [part.astype(F32) for part in parts]
        mine = jnp.concatenate([
            jnp.where(lane == TILE - 1, rot(parts[0], TILE - 1 - edge), rot(parts[1], 2 * TILE - 2 - edge)),
            near_out[side].astype(F32),
            jnp.where(lane == 0, rot(parts[2], TILE - edge), rot(parts[3], TILE + 1 - edge))], axis=1)
        outer = jnp.where(polars[side], mine, far)
        inner = jnp.where(polars[side], far, mine)
        order = (outer, near, inner) if side == 0 else (inner, near, outer)
        for e in range(3):
            for a in range(3):
                at = (3 * a + e) * CL
                strip[at:at + CL, :] = rot(order[e], 1 - a).astype(BF16)
        gates = jnp.dot(
            wle[:, 0:9 * CL + 16],
            jnp.concatenate([strip[...], jnp.ones((16, 3 * TILE), BF16)], axis=0),
            preferred_element_type=F32,
        )
        west, east = west[0:HID], east[0:HID]
        cell = jnp.concatenate([
            rot(west, TILE - 6) + rot(west, TILE - 7) + rot(west, TILE - 8),
            cell_in[side],
            rot(east, TILE - 5) + rot(east, TILE - 6) + rot(east, TILE - 7)], axis=1)
        hs[side], _ = update(gates, cell)

    for k, tile in enumerate(interleaved(hs[0, :, TILE:2 * TILE], hs[1, :, TILE:2 * TILE])):
        g_top[k, 0:HID] = tile.astype(BF16)
    for k, tile in enumerate(interleaved(rest_in[0, CL:PA].astype(F32), rest_in[1, CL:PA].astype(F32))):
        g_top[k, HID:CT] = tile.astype(BF16)

    hidden, _ = update(windows(s_low, 0, 129, 9 * CL, wle), jnp.concatenate([lonf_in[0], lonf_in[1]], axis=1))
    for side in range(2):
        src = TILE - 1 if side == 0 else 0
        value = hidden[:, side * TILE:(side + 1) * TILE]
        lo = rot(hs[0, :, 2 * side * TILE:(2 * side + 1) * TILE], TILE - src)
        hi = rot(hs[1, :, 2 * side * TILE:(2 * side + 1) * TILE], 2 * TILE - 1 - src)
        sp[side, CT:CT + HID] = value.astype(BF16)
        shifted(sp, side, 0, HID, CT, value, lo, hi)
        value = lonb_in[side, 2 * CL:PK].astype(F32)
        lo = rot(cor_in[0, side, 0:HID].astype(F32), TILE - 4)
        hi = rot(cor_in[1, side, 0:HID].astype(F32), TILE - 5)
        sp[side, CT + HID:2 * CT] = value.astype(BF16)
        shifted(sp, side, HID, HID, CT, value, lo, hi)

    for copy in copies:
        copy.wait_send()
    for b in range(NB):
        for save in save_block(b):
            save.wait()
    saves[0].wait()


def lower_layer(fr, hl, ht, cl, wl, bl):
    anywhere = pl.BlockSpec(memory_space=pl.ANY)
    whole = pl.BlockSpec(memory_space=pltpu.VMEM)
    exchanged = [
        pltpu.VMEM((2, CL, TILE), BF16),
        pltpu.VMEM((2, PA, TILE), BF16),
        pltpu.VMEM((2, HID, TILE), F32),
        pltpu.VMEM((2, 2, CL, TILE), BF16),
        pltpu.VMEM((2, PK, TILE), BF16),
        pltpu.VMEM((2, HID, TILE), F32),
    ]
    return pl.pallas_call(
        lower_kernel,
        out_shape=(
            jax.ShapeDtypeStruct((TILE, HID, TILE), BF16),
            jax.ShapeDtypeStruct((TILE, HID, TILE), BF16),
            jax.ShapeDtypeStruct((NB, HID, BX, TILE), F32),
            jax.ShapeDtypeStruct((2, CT, TILE), BF16),
            jax.ShapeDtypeStruct((2, 3 * CT, TILE), BF16),
        ),
        in_specs=[anywhere] * 4 + [whole] * 2,
        out_specs=(anywhere, anywhere, anywhere, whole, whole),
        scratch_shapes=[
            pltpu.VMEM((CIN, TILE, TILE), BF16),
            pltpu.VMEM((HID, TILE, TILE), BF16),
            pltpu.VMEM((HID, TILE, TILE), BF16),
            pltpu.VMEM((NB, HID, PITCH, TILE), F32),
            pltpu.VMEM((TILE + 4, 3 * CL, TILE), BF16),
            pltpu.VMEM((2, TILE, HID, TILE), BF16),
            pltpu.VMEM((9 * CL, 3 * TILE), BF16),
            pltpu.VMEM((2, HID, 3 * TILE), F32),
            pltpu.VMEM((2, CL, TILE), BF16),
            pltpu.VMEM((4 * HID, 9 * CL + 48), BF16),
            pltpu.VMEM((HID * BX, TILE), F32),
            pltpu.VMEM((HID * 8, TILE), F32),
            *exchanged,
            *exchanged,
            pltpu.SemaphoreType.DMA((3 + NB + HID // CIN,)),
            pltpu.SemaphoreType.DMA((3, NB)),
            pltpu.SemaphoreType.DMA((3, 2)),
            pltpu.SemaphoreType.DMA((3, 2)),
            pltpu.SemaphoreType.DMA((2, 2)),
            pltpu.SemaphoreType.DMA((2, 2)),
            pltpu.SemaphoreType.DMA((2, 2)),
            pltpu.SemaphoreType.DMA((2, 2)),
        ],
        compiler_params=pltpu.CompilerParams(
            collective_id=0, has_side_effects=True, vmem_limit_bytes=60 * 1024 * 1024
        ),
        name="lower_layer",
    )(fr, hl, ht, cl, wl, bl)


def upper_kernel(
    t_hid, t_ht, co_in, ct, g_top, sp, wt, bt,
    th, ho, co, cto,
    ctv, cov, hov, thv, s_top, wte, rows,
    sem_in, sem_out,
):
    def span(b):
        return pl.ds(pl.multiple_of(b * BX, BX), BX)

    def load(k, b):
        if k >= 2:
            source, dest = (ct.at[:, span(b), :], ctv.at[b, :, 0:BX, :]) if k == 2 else (co_in.at[b], cov.at[b])
            return pltpu.make_async_copy(source, dest, sem_in.at[k, b])
        source = (t_hid, t_ht)[k]
        at = CT + k * HID
        return pltpu.make_async_copy(
            source.at[span(b)], s_top.at[pl.ds(b * BX + 1, BX), at:at + HID, :], sem_in.at[k, b])

    def save(k, b):
        source, dest = ((hov, ho), (thv, th), (ctv, cto), (cov, co))[k]
        source = source.at[b, :, 0:BX, :] if k == 2 else source.at[b]
        return pltpu.make_async_copy(source, dest.at[:, span(b), :], sem_out.at[k, b])

    for b in range(2):
        for k in range(4):
            load(k, b).start()

    extended_weights(wte, wt[...].astype(F32), bt[...], 9 * CT)
    s_top[0] = sp[0]
    s_top[TILE + 1] = sp[1]

    def shift_row(x, parity):
        halo = rot(g_top[parity].astype(F32), lax.rem(TILE - x, TILE))
        shifted(s_top, x + 1, 0, CT, CT, s_top[x + 1, CT:2 * CT].astype(F32), halo, halo)

    for k in range(2):
        load(k, 0).wait()
    for b in range(2, 4):
        for k in range(4):
            load(k, b).start()

    for row in range(AHEAD):
        shift_row(row, row % 2)

    def top_rows(b, i, shift):
        x = b * BX + i
        cells = ctv.at[b].reshape(HID * PITCH, TILE)
        cell = jnp.concatenate([cells[pl.ds(i + j, HID, stride=PITCH), :] for j in range(2)], axis=1)
        hidden, cell = update(windows(s_top, x, x + 1, 9 * CT, wte), cell)
        for j in range(2):
            if shift or i + AHEAD < BX:
                shift_row(x + AHEAD + j, j)
            part = slice(j * TILE, (j + 1) * TILE)
            cells[pl.ds(i + j, HID, stride=PITCH), :] = cell[:, part]
            rows[i + j] = hidden[:, part].astype(BF16)

    def top_block(b, shift, before):
        hov[b] = jnp.swapaxes(s_top[pl.ds(b * BX + 1, BX), CT:CT + HID], 0, 1)
        thv[before] = jnp.swapaxes(rows[...], 0, 1)
        for i in range(0, BX, 2):
            top_rows(b, i, shift)
        for k in (0, 2, 3):
            save(k, b).start()

    def arrived(k, b):
        for kind in k:
            load(kind, b).wait()

    def top_step(step, carry):
        b = 2 * step

        @pl.when(step > 0)
        def _():
            save(1, b - 2).start()

        @pl.when(b + 4 < NB)
        def _():
            for k in range(4):
                load(k, b + 4).start()
                load(k, b + 5).start()

        arrived((2, 3), b)
        arrived((0, 1), b + 1)
        before = jnp.maximum(b - 1, 0)
        top_block(b, True, before)
        arrived((2, 3), b + 1)
        arrived((0, 1), b + 2)
        top_block(b + 1, True, b)

        @pl.when(step > 0)
        def _():
            save(1, b - 1).start()
        return carry

    rows[...] = jnp.zeros(rows.shape, BF16)
    lax.fori_loop(0, NB // 2 - 1, top_step, 0)
    b = NB - 2
    save(1, b - 2).start()
    arrived((2, 3), b)
    arrived((0, 1, 2, 3), b + 1)
    top_block(b, True, b - 1)
    save(1, b - 1).start()
    top_block(b + 1, False, b)
    save(1, b).start()
    thv[b + 1] = jnp.swapaxes(rows[...], 0, 1)
    save(1, b + 1).start()
    for k in range(4):
        for b in range(NB):
            save(k, b).wait()


def upper_layer(t_hid, t_ht, co, ct, g_top, sp, wt, bt):
    anywhere = pl.BlockSpec(memory_space=pl.ANY)
    whole = pl.BlockSpec(memory_space=pltpu.VMEM)
    field = (HID, TILE, TILE)
    return pl.pallas_call(
        upper_kernel,
        out_shape=(
            jax.ShapeDtypeStruct(field, BF16),
            jax.ShapeDtypeStruct(field, BF16),
            jax.ShapeDtypeStruct(field, F32),
            jax.ShapeDtypeStruct(field, F32),
        ),
        in_specs=[anywhere] * 4 + [whole] * 4,
        out_specs=(anywhere,) * 4,
        scratch_shapes=[
            pltpu.VMEM((NB, HID, PITCH, TILE), F32),
            pltpu.VMEM((NB, HID, BX, TILE), F32),
            pltpu.VMEM((NB, HID, BX, TILE), BF16),
            pltpu.VMEM((NB, HID, BX, TILE), BF16),
            pltpu.VMEM((TILE + 2, 3 * CT, TILE), BF16),
            pltpu.VMEM((4 * HID, 9 * CT + TILE), BF16),
            pltpu.VMEM((BX, HID, TILE), BF16),
            pltpu.SemaphoreType.DMA((4, NB)),
            pltpu.SemaphoreType.DMA((4, NB)),
        ],
        compiler_params=pltpu.CompilerParams(vmem_limit_bytes=60 * 1024 * 1024),
        name="upper_layer",
    )(t_hid, t_ht, co, ct, g_top, sp, wt, bt)


def body(frames, hidden_low, cell_low, hidden_top, cell_top, weight_low, bias_low, weight_top, bias_top):
    fr = frames.reshape(frames.shape[2:])
    hl, cl, ht, ct = (field.reshape(field.shape[1:]) for field in (hidden_low, cell_low, hidden_top, cell_top))
    t_hid, t_ht, co, g_top, sp = lower_layer(fr, hl, ht, cl, weight_low.T, bias_low.reshape(1, -1))
    th, ho, co, cto = upper_layer(t_hid, t_ht, co, ct, g_top, sp, weight_top, bias_top.reshape(1, -1))
    return th[None, None], ho[None], co[None], cto[None]


def solution(mesh):
    field = P(None, None, "lon", "lat")
    frame = P(None, None, None, "lon", "lat")
    return jax.shard_map(
        body,
        mesh=mesh,
        in_specs=(frame, field, field, field, field, P(), P(), P(), P()),
        out_specs=(frame, field, field, field),
        check_vma=False,
    )
```
